32 devices in a mesh: gz: 4 (over x, core), gy: 8 (over z, y).
Axes of the slice: x: 2, y: 2, z: 4, core: 2. Of those that a mesh axis runs over, the one named last changes fastest.
Arguments:
- velocity: float32 [3, 256, 256, 512], P(None, None, 'gy', 'gz'), may hold values from -0.3 to 0.3
- increment: float32 [3, 256, 256, 512], P(None, None, 'gy', 'gz'), may hold values from -4 to 4
- template: bfloat16 [256, 256, 512], P(None, 'gy', 'gz'), may hold values from 0 to 1
- deformed: bfloat16 [256, 256, 512], P(None, 'gy', 'gz'), may hold values from 0 to 1
Outputs:
- preconditioned: float32 [3, 256, 256, 512], P(None, None, 'gy', 'gz')
The draws below stay inside these ranges and needn't reach their ends.
All inputs are finite; a program needn't handle non-finite values.
Results may differ from the reference program's by a relative error of at most 0.0003.
Values sent between devices are 32-bit elements; how exact they have to be, the bound alone decides.
No kernel may reach another device: no remote copies, remote signals or barrier semaphores. Data moves between devices by JAX's collectives and lax.ppermute only.
A program may use at most 576 MiB of HBM per device.

```python
import math
import jax
import jax.numpy as jnp
from jax import lax

NX = 256
NY = 256
NZ = 512


def block_scale(stream_key, shape, shards, least, high):
    def one(axis_at, parts):
        steps = jax.random.uniform(jax.random.fold_in(jax.random.fold_in(stream_key, 6), axis_at), (parts,), jnp.float32, least / len(shards), high / len(shards))
        return jnp.repeat(jnp.exp(steps), shape[axis_at] // parts).reshape((-1,) + (1,) * (len(shape) - axis_at - 1))

    level = one(*shards[0])
    for cut in shards[1:]:
        level = level * one(*cut)
    return level


def bell_draw(stream_key, shape, scale, most, split=(), kind=jnp.bfloat16):
    drawn = jax.random.normal(stream_key, shape, jnp.float32) * scale
    if len(split) > 0:
        drawn = block_scale(stream_key, shape, split, -0.22, 0.18) * drawn
    return jnp.clip(drawn, min=-most, max=most).astype(kind)


def setup_inputs(seed: int = 0) -> dict:
    key_of = jax.random.split(jax.random.key(seed), 5)
    return {
        "velocity": jnp.clip(jax.random.uniform(key_of[0], (3, NX, NY, NZ), jnp.float32, -0.3, 0.3) * block_scale(key_of[0], (3, NX, NY, NZ), ((2, 8), (3, 4)), -0.4, 0.0), -0.3, 0.3),
        "increment": bell_draw(key_of[1], (3, NX, NY, NZ), 1.0, 4.0, ((2, 8), (3, 4)), jnp.float32),
        "template": jnp.clip(1.0 * jax.random.uniform(key_of[2], (NX, NY, NZ), jnp.float32) ** block_scale(key_of[2], (NX, NY, NZ), ((1, 8), (2, 4)), -0.2, 0.2), 0.0, 1.0).astype(jnp.bfloat16),
        "deformed": jnp.clip(1.0 * jax.random.uniform(key_of[3], (NX, NY, NZ), jnp.float32) ** block_scale(key_of[3], (NX, NY, NZ), ((1, 8), (2, 4)), -0.2, 0.2), 0.0, 1.0).astype(jnp.bfloat16),
    }


STEP = 0.5
BETA = 0.02
GAMMA = 0.05
COARSE_BETA = 0.025
OMEGA = 1.0 / (0.05 + 42.0 * 0.02)


def cas_table(count):
    index = jnp.arange(count, dtype=jnp.int32)
    product = (index[:, None] * index[None, :]) % count
    angle = product.astype(jnp.float32) * (2.0 * math.pi / count)
    return jnp.cos(angle) + jnp.sin(angle)


def eigen_line(count):
    index = jnp.arange(count, dtype=jnp.int32).astype(jnp.float32)
    return 2.0 - 2.0 * jnp.cos(index * (2.0 * math.pi / count))


def filtered(field, gamma, beta, inverse):
    nx, ny, nz = field.shape[1], field.shape[2], field.shape[3]
    table_x, table_y, table_z = cas_table(nx), cas_table(ny), cas_table(nz)
    total = eigen_line(nx)[:, None, None] + eigen_line(ny)[None, :, None] + eigen_line(nz)[None, None, :]
    symbol = gamma + beta * total * total
    high = lax.Precision.HIGHEST

    def one(part):
        coeffs = jnp.einsum('xi,ijk->xjk', table_x, part, precision=high)
        coeffs = jnp.einsum('yj,xjk->xyk', table_y, coeffs, precision=high)
        coeffs = jnp.einsum('zk,xyk->xyz', table_z, coeffs, precision=high)
        if inverse:
            coeffs = coeffs / symbol
        else:
            coeffs = coeffs * symbol
        coeffs = jnp.einsum('xi,ijk->xjk', table_x, coeffs, precision=high)
        coeffs = jnp.einsum('yj,xjk->xyk', table_y, coeffs, precision=high)
        coeffs = jnp.einsum('zk,xyk->xyz', table_z, coeffs, precision=high)
        return coeffs / float(nx * ny * nz)

    return lax.map(one, field)


def plus(field, axis):
    return jnp.roll(field, -1, axis)


def minus(field, axis):
    return jnp.roll(field, 1, axis)


def expand(field):
    return jnp.repeat(jnp.repeat(jnp.repeat(field, 4, axis=1), 4, axis=2), 4, axis=3)


def reference(velocity, increment, template, deformed):
    first = template.astype(jnp.float32)
    second = deformed.astype(jnp.float32)
    grad_first = [0.5 * (plus(first, d) - minus(first, d)) for d in range(3)]
    grad_second = [0.5 * (plus(second, d) - minus(second, d)) for d in range(3)]
    state_one = -STEP * (increment[0] * grad_first[0] + increment[1] * grad_first[1] + increment[2] * grad_first[2])
    advect = jnp.zeros_like(state_one)
    for d in range(3):
        advect = advect + jnp.maximum(velocity[d], 0.0) * (state_one - minus(state_one, d))
        advect = advect + jnp.minimum(velocity[d], 0.0) * (plus(state_one, d) - state_one)
    source = increment[0] * grad_second[0] + increment[1] * grad_second[1] + increment[2] * grad_second[2]
    state_two = state_one - STEP * (advect + source)
    adjoint_two = -state_two
    change = jnp.zeros_like(adjoint_two)
    for d in range(3):
        outflow = jnp.maximum(velocity[d], 0.0) * adjoint_two
        inflow = jnp.minimum(velocity[d], 0.0) * adjoint_two
        change = change + (inflow - minus(inflow, d)) + (plus(outflow, d) - outflow)
    adjoint_one = adjoint_two + STEP * change
    force = jnp.stack([STEP * (adjoint_one * grad_first[d] + adjoint_two * grad_second[d]) for d in range(3)])
    hessian = filtered(increment, GAMMA, BETA, False) + force
    nx, ny, nz = hessian.shape[1], hessian.shape[2], hessian.shape[3]
    restricted = jnp.mean(hessian.reshape(3, nx // 4, 4, ny // 4, 4, nz // 4, 4), axis=(2, 4, 6))
    coarse = filtered(restricted, GAMMA, COARSE_BETA, True)
    return expand(coarse) + OMEGA * (hessian - expand(restricted))
```

```python
import functools
import math

import jax
import jax.numpy as jnp
from jax import lax
from jax.experimental import pallas as pl
from jax.experimental.pallas import tpu as pltpu
from jax.sharding import PartitionSpec as P

STEP = 0.5
BETA = 0.02
GAMMA = 0.05
COARSE_BETA = 0.025
OMEGA = 1.0 / (0.05 + 42.0 * 0.02)
HIGH = lax.Precision.HIGHEST

PART = 32
GROUP = 4
LANES = 128
TOP = 8
PAIR = 2


def shifted(value, axis, by):
    peers = lax.axis_size(axis)
    return lax.ppermute(value, axis, [(i, (i + by) % peers) for i in range(peers)])


def cas_table(count):
    index = jnp.arange(count, dtype=jnp.int32)
    product = index[:, None] * index[None, :] % count
    angle = product.astype(jnp.float32) * (2.0 * math.pi / count)
    return jnp.cos(angle) + jnp.sin(angle)


def eigen_line(count):
    index = jnp.arange(count, dtype=jnp.int32).astype(jnp.float32)
    return 2.0 - 2.0 * jnp.cos(index * (2.0 * math.pi / count))


def lane_of(rows):
    return lax.broadcasted_iota(jnp.int32, (rows, LANES), 1)


def turn(value, by):
    return pltpu.roll(value, by % LANES if isinstance(by, int) else by, 1)


def turned_to(value, place):
    return pltpu.roll(value, lax.rem(place, LANES), 1)


def turned_from(value, place):
    return pltpu.roll(value, lax.rem(LANES - lax.rem(place, LANES), LANES), 1)


def z_sides(value, rim, lane):
    before = turn(jnp.where(lane == LANES - 1, rim, value), 1)
    after = turn(jnp.where(lane == 0, rim, value), -1)
    return before, after


def planes_loop(count, body, carry=0, step=PAIR):
    def several(k, carry):
        for j in range(step):
            carry = body(k * step + j, carry)
        return carry

    return lax.fori_loop(0, count // step, several, carry)


def call(body, grid, in_specs, out_specs, out_shape, scratch, flops, moved):
    return pl.pallas_call(
        body,
        grid=grid,
        in_specs=in_specs,
        out_specs=out_specs,
        out_shape=out_shape,
        scratch_shapes=scratch,
        cost_estimate=pl.CostEstimate(flops=flops, bytes_accessed=moved, transcendentals=0),
        compiler_params=pltpu.CompilerParams(
            vmem_limit_bytes=48 * 1024 * 1024,
            dimension_semantics=("arbitrary",) * len(grid),
        ),
    )


def f32(*shape):
    return jax.ShapeDtypeStruct(shape, jnp.float32)


def state_rims_body(first, second, packed, low0, low1, high0, high1):
    rows = first.shape[1]
    lane = lane_of(rows)
    owner = lane // GROUP
    spot = lane % GROUP

    def plane(i, edge):
        a = first[i].astype(jnp.float32)
        b = second[i].astype(jnp.float32)
        low0[pl.ds(i, 1), :] = a[:1]
        low1[pl.ds(i, 1), :] = b[:1]
        high0[pl.ds(i, 1), :] = a[rows - 1 :]
        high1[pl.ds(i, 1), :] = b[rows - 1 :]
        both = jnp.where(spot < 2, turned_to(a, GROUP * i + 1), turned_to(b, GROUP * i + 3))
        return jnp.where(owner == i, both, edge)

    packed[...] = planes_loop(PART, plane, jnp.zeros((rows, LANES), jnp.float32))


def state_rims(first, second):
    xlen, rows = first.shape[0], first.shape[1]
    block = pl.BlockSpec((PART, rows, LANES), lambda i: (i, 0, 0))
    slab = pl.BlockSpec((PART, LANES), lambda i: (i, 0))
    return call(
        state_rims_body,
        (xlen // PART,),
        [block, block],
        [pl.BlockSpec((rows, LANES), lambda i: (0, i))] + [slab] * 4,
        [f32(rows, GROUP * xlen)] + [f32(xlen, LANES)] * 4,
        [],
        8 * first.size,
        4 * first.size,
    )(first, second)


def stencil_body(before, cells, after, out, packed, padded, inner):
    rows = cells.shape[2]
    lane = lane_of(rows)
    owner = lane // GROUP
    here = pl.ds(TOP, rows)

    @pl.when((pl.program_id(0) == 0) & (pl.program_id(1) == 0))
    def _():
        padded[...] = jnp.zeros_like(padded)

    for j in range(2):
        padded[j, here] = before[0, j]
        padded[PART + 2 + j, here] = after[0, j]

    def fill(i, carry):
        padded[i + 2, here] = cells[0, i]
        return carry

    planes_loop(PART, fill)

    def middle(j):
        value = padded[j, here]
        near = turn(jnp.where(lane == LANES - 1, 0.0, value), 1) + turn(
            jnp.where(lane == 0, 0.0, value), -1
        )
        core = near - 6.0 * value
        around = (
            padded[j - 1, here]
            + padded[j + 1, here]
            + padded[j, TOP - 1 : TOP - 1 + rows]
            + padded[j, TOP + 1 : TOP + 1 + rows]
        )
        inner[j - 1, here] = core + 0.5 * around
        inner[j - 1, TOP - 1 : TOP] = 0.5 * value[:1]
        inner[j - 1, TOP + rows : TOP + rows + 1] = 0.5 * value[rows - 1 :]
        return value, core

    middle(1)
    middle(PART + 2)

    def plane(i, edge):
        value, core = middle(i + 2)
        far = turn(jnp.where(lane >= LANES - 2, 0.0, value), 2) + turn(
            jnp.where(lane < 2, 0.0, value), -2
        )
        out[0, i] = BETA * far - (12.0 * BETA) * core + (GAMMA - 34.0 * BETA) * value
        return jnp.where(owner == i, turned_to(value, GROUP * i + 2), edge)

    packed[0] = planes_loop(PART, plane, jnp.zeros((rows, LANES), jnp.float32))

    def finish(i, carry):
        around = (
            inner[i, here]
            + inner[i + 2, here]
            + inner[i + 1, TOP - 1 : TOP - 1 + rows]
            + inner[i + 1, TOP + 1 : TOP + 1 + rows]
        )
        out[0, i] = out[0, i] + (2.0 * BETA) * around
        return carry

    planes_loop(PART, finish)


def stencil(increment):
    parts, xlen, rows = increment.shape[:3]
    half = PART // 2
    pairs = xlen // 2
    block = pl.BlockSpec((1, PART, rows, LANES), lambda c, i: (c, i, 0, 0))
    return call(
        stencil_body,
        (parts, xlen // PART),
        [
            pl.BlockSpec(
                (1, 2, rows, LANES), lambda c, i: (c, lax.rem(half * i + pairs - 1, pairs), 0, 0)
            ),
            block,
            pl.BlockSpec(
                (1, 2, rows, LANES), lambda c, i: (c, lax.rem(half * i + half, pairs), 0, 0)
            ),
        ],
        [block, pl.BlockSpec((1, rows, LANES), lambda c, i: (c, 0, i))],
        [f32(parts, xlen, rows, LANES), f32(parts, rows, GROUP * xlen)],
        [
            pltpu.VMEM((PART + 4, rows + 2 * TOP, LANES), jnp.float32),
            pltpu.VMEM((PART + 2, rows + 2 * TOP, LANES), jnp.float32),
        ],
        24 * increment.size,
        8 * increment.size,
    )(increment, increment, increment)


def gradient(ref, before, after, i, low, high, rim, buffer, lane):
    rows = ref.shape[1]
    value = ref[i].astype(jnp.float32)
    buffer[TOP : TOP + rows] = value
    buffer[TOP - 1 : TOP] = low[pl.ds(i, 1), :]
    buffer[TOP + rows : TOP + rows + 1] = high[pl.ds(i, 1), :]
    prev = jnp.where(i == 0, before[0], ref[jnp.maximum(i - 1, 0)]).astype(jnp.float32)
    later = jnp.where(i == PART - 1, after[0], ref[jnp.minimum(i + 1, PART - 1)]).astype(
        jnp.float32
    )
    left, right = z_sides(value, rim, lane)
    return (
        later - prev,
        buffer[TOP + 1 : TOP + 1 + rows] - buffer[TOP - 1 : TOP - 1 + rows],
        right - left,
    )


def merged_rims(left, right, rows):
    spot = lane_of(rows) % GROUP
    return jnp.where(spot % 2 == 0, left[...], right[...])


def first_state_body(
    increment, m0, m0b, m0a, m1, m1b, m1a, low0, low1, high0, high1, left, right,
    state, source, packed, low, high, pad0, pad1,
):
    rows = m0.shape[1]
    lane = lane_of(rows)
    owner = lane // GROUP
    rims = merged_rims(left, right, rows)

    def plane(i, edge):
        g0 = gradient(
            m0, m0b, m0a, i, low0, high0, turned_from(rims, GROUP * i + 1), pad0.at[i % PAIR], lane
        )
        g1 = gradient(
            m1, m1b, m1a, i, low1, high1, turned_from(rims, GROUP * i + 3), pad1.at[i % PAIR], lane
        )
        u = [increment[d, i] for d in range(3)]
        one = (-0.5 * STEP) * (u[0] * g0[0] + u[1] * g0[1] + u[2] * g0[2])
        state[i] = one
        source[i] = (0.5 * STEP) * (u[0] * g1[0] + u[1] * g1[1] + u[2] * g1[2])
        low[pl.ds(i, 1), :] = one[:1]
        high[pl.ds(i, 1), :] = one[rows - 1 :]
        return jnp.where(owner == i, turned_to(one, GROUP * i + 1), edge)

    packed[...] = planes_loop(PART, plane, jnp.zeros((rows, LANES), jnp.float32))


def around_specs(xlen, rows):
    return [
        pl.BlockSpec((PART, rows, LANES), lambda i: (i, 0, 0)),
        pl.BlockSpec((1, rows, LANES), lambda i: (lax.rem(PART * i + xlen - 1, xlen), 0, 0)),
        pl.BlockSpec((1, rows, LANES), lambda i: (lax.rem(PART * i + PART, xlen), 0, 0)),
    ]


def first_state(increment, first, second, slabs, left, right):
    xlen, rows = first.shape[0], first.shape[1]
    triple = pl.BlockSpec((3, PART, rows, LANES), lambda i: (0, i, 0, 0))
    block = pl.BlockSpec((PART, rows, LANES), lambda i: (i, 0, 0))
    slab = pl.BlockSpec((PART, LANES), lambda i: (i, 0))
    rim = pl.BlockSpec((rows, LANES), lambda i: (0, i))
    return call(
        first_state_body,
        (xlen // PART,),
        [triple] + around_specs(xlen, rows) * 2 + [slab] * 4 + [rim, rim],
        [block, block, rim, slab, slab],
        [f32(xlen, rows, LANES)] * 2 + [f32(rows, GROUP * xlen)] + [f32(xlen, LANES)] * 2,
        [pltpu.VMEM((PAIR, rows + 2 * TOP, LANES), jnp.float32)] * 2,
        24 * first.size,
        24 * first.size,
    )(increment, first, first, first, second, second, second, *slabs, left, right)


def second_state_body(
    velocity, source, state, state_b, state_a, low, high, left, right,
    adjoint, packed, out_low, out_high, pad,
):
    rows = state.shape[1]
    lane = lane_of(rows)
    owner = lane // GROUP
    rims = merged_rims(left, right, rows)

    def plane(i, edge):
        value = state[i]
        buffer = pad.at[i % PAIR]
        buffer[TOP : TOP + rows] = value
        buffer[TOP - 1 : TOP] = low[pl.ds(i, 1), :]
        buffer[TOP + rows : TOP + rows + 1] = high[pl.ds(i, 1), :]
        prev = jnp.where(i == 0, state_b[0], state[jnp.maximum(i - 1, 0)])
        later = jnp.where(i == PART - 1, state_a[0], state[jnp.minimum(i + 1, PART - 1)])
        sides = [
            (prev, later),
            (buffer[TOP - 1 : TOP - 1 + rows], buffer[TOP + 1 : TOP + 1 + rows]),
            z_sides(value, turned_from(rims, GROUP * i + 1), lane),
        ]
        total = source[i] - value
        for d in range(3):
            speed = velocity[d, i]
            slope = jnp.where(speed > 0.0, value - sides[d][0], sides[d][1] - value)
            total = total + (STEP * speed) * slope
        adjoint[i] = total
        along = velocity[1, i]
        out_low[pl.ds(i, 1), :] = jnp.maximum(along[:1], 0.0) * total[:1]
        out_high[pl.ds(i, 1), :] = jnp.minimum(along[rows - 1 :], 0.0) * total[rows - 1 :]
        along = velocity[2, i]
        across = total * jnp.where(
            lane == LANES - 1, jnp.minimum(along, 0.0), jnp.maximum(along, 0.0)
        )
        return jnp.where(owner == i, turned_to(across, GROUP * i + 1), edge)

    packed[...] = planes_loop(PART, plane, jnp.zeros((rows, LANES), jnp.float32))


def second_state(velocity, source, state, low, high, left, right):
    xlen, rows = state.shape[0], state.shape[1]
    triple = pl.BlockSpec((3, PART, rows, LANES), lambda i: (0, i, 0, 0))
    block = pl.BlockSpec((PART, rows, LANES), lambda i: (i, 0, 0))
    slab = pl.BlockSpec((PART, LANES), lambda i: (i, 0))
    rim = pl.BlockSpec((rows, LANES), lambda i: (0, i))
    return call(
        second_state_body,
        (xlen // PART,),
        [triple, block] + around_specs(xlen, rows) + [slab, slab, rim, rim],
        [block, rim, slab, slab],
        [f32(xlen, rows, LANES), f32(rows, GROUP * xlen)] + [f32(xlen, LANES)] * 2,
        [pltpu.VMEM((PAIR, rows + 2 * TOP, LANES), jnp.float32)],
        30 * state.size,
        24 * state.size,
    )(velocity, source, state, state, state, low, high, left, right)


def hessian_body(
    filtered, velocity, speed_b, speed_a, adjoint, adjoint_b, adjoint_a,
    m0, m0b, m0a, m1, m1b, m1a, low0, low1, high0, high1, left, right,
    flow_low, flow_high, flow_left, flow_right, edge_low, edge_high, edge_lanes, fold_y, fold_z,
    out, restricted, pad0, pad1, pad2, pad3, sums,
):
    rows = m0.shape[1]
    lane = lane_of(rows)
    rims = merged_rims(left, right, rows)
    flows = merged_rims(flow_left, flow_right, rows)
    outer = (lane < 2) | (lane >= LANES - 2)

    def plane(i, carry):
        slot = i % PAIR
        g0 = gradient(
            m0, m0b, m0a, i, low0, high0, turned_from(rims, GROUP * i + 1), pad0.at[slot], lane
        )
        g1 = gradient(
            m1, m1b, m1a, i, low1, high1, turned_from(rims, GROUP * i + 3), pad1.at[slot], lane
        )
        value = adjoint[i]
        sx, sy, sz = (velocity[d, i] for d in range(3))
        kept = jnp.abs(sx) + jnp.abs(sy) + jnp.abs(sz)
        before, after = jnp.maximum(i - 1, 0), jnp.minimum(i + 1, PART - 1)
        prev = jnp.where(
            i == 0,
            jnp.minimum(speed_b[0, 0], 0.0) * adjoint_b[0],
            jnp.minimum(velocity[0, before], 0.0) * adjoint[before],
        )
        later = jnp.where(
            i == PART - 1,
            jnp.maximum(speed_a[0, 0], 0.0) * adjoint_a[0],
            jnp.maximum(velocity[0, after], 0.0) * adjoint[after],
        )
        change = later - prev
        inflow = pad2.at[slot]
        outflow = pad3.at[slot]
        inflow[TOP : TOP + rows] = jnp.minimum(sy, 0.0) * value
        inflow[TOP - 1 : TOP] = flow_low[pl.ds(i, 1), :]
        outflow[TOP : TOP + rows] = jnp.maximum(sy, 0.0) * value
        outflow[TOP + rows : TOP + rows + 1] = flow_high[pl.ds(i, 1), :]
        change = change + (
            outflow[TOP + 1 : TOP + 1 + rows] - inflow[TOP - 1 : TOP - 1 + rows]
        )
        rim = turned_from(flows, GROUP * i + 1)
        change = change + turn(
            jnp.where(lane == 0, rim, jnp.maximum(sz, 0.0) * value), -1
        )
        change = change - turn(
            jnp.where(lane == LANES - 1, rim, jnp.minimum(sz, 0.0) * value), 1
        )
        half_two = (0.5 * STEP) * value
        half_one = half_two + (0.5 * STEP * STEP) * (change - kept * value)
        for d in range(3):
            cyclic = turned_from(edge_lanes[d], GROUP * i + 2)
            out[d, i] = (
                filtered[d, i]
                + jnp.where(outer, cyclic, 0.0)
                + half_one * g0[d]
                + half_two * g1[d]
            )
            out[d, i, 0:2] = out[d, i, 0:2] + edge_low[d, pl.ds(2 * i, 2), :]
            out[d, i, rows - 2 : rows] = out[d, i, rows - 2 : rows] + edge_high[d, pl.ds(2 * i, 2), :]
        return carry

    planes_loop(PART, plane)

    for d in range(3):

        def fold(k, carry):
            sums[k] = (out[d, 4 * k] + out[d, 4 * k + 1]) + (out[d, 4 * k + 2] + out[d, 4 * k + 3])
            return carry

        lax.fori_loop(0, PART // 4, fold, 0)
        block = sums[...].reshape(PART // 4 * rows, LANES)
        block = jnp.dot(block, fold_z[...], precision=HIGH, preferred_element_type=jnp.float32)
        block = jnp.dot(fold_y[...], block, precision=HIGH, preferred_element_type=jnp.float32)
        restricted[d] = block * (1.0 / 64.0)


def hessian_pass(
    filtered, velocity, adjoint, first, second, slabs, left, right, flow_low, flow_high, flow_left,
    flow_right, edge_low, edge_high, edge_lanes, fold_y, fold_z,
):
    xlen, rows = first.shape[0], first.shape[1]
    triple = pl.BlockSpec((3, PART, rows, LANES), lambda i: (0, i, 0, 0))
    slab = pl.BlockSpec((PART, LANES), lambda i: (i, 0))
    rim = pl.BlockSpec((rows, LANES), lambda i: (0, i))
    rows_two = pl.BlockSpec((3, 2 * PART, LANES), lambda i: (0, i, 0))
    whole = lambda a: pl.BlockSpec(a.shape, lambda i: (0, 0))
    coarse_rows = PART // 4 * (rows // 4)
    around = around_specs(xlen, rows)
    pad = pltpu.VMEM((PAIR, rows + 2 * TOP, LANES), jnp.float32)
    return call(
        hessian_body,
        (xlen // PART,),
        [
            triple,
            triple,
            pl.BlockSpec(
                (1, 1, rows, LANES), lambda i: (0, lax.rem(PART * i + xlen - 1, xlen), 0, 0)
            ),
            pl.BlockSpec((1, 1, rows, LANES), lambda i: (0, lax.rem(PART * i + PART, xlen), 0, 0)),
        ]
        + around * 3
        + [slab] * 4
        + [rim, rim, slab, slab, rim, rim, rows_two, rows_two]
        + [pl.BlockSpec((3, rows, LANES), lambda i: (0, 0, i)), whole(fold_y), whole(fold_z)],
        [triple, pl.BlockSpec((3, coarse_rows, LANES // 4), lambda i: (0, i, 0))],
        [f32(3, xlen, rows, LANES), f32(3, xlen // 4 * (rows // 4), LANES // 4)],
        [pad, pad, pad, pad, pltpu.VMEM((PART // 4, rows, LANES), jnp.float32)],
        90 * first.size,
        48 * first.size,
    )(
        filtered, velocity, velocity, velocity, adjoint, adjoint, adjoint,
        first, first, first, second, second, second, *slabs, left, right,
        flow_low, flow_high, flow_left, flow_right, edge_low, edge_high, edge_lanes, fold_y, fold_z,
    )


def final_body(hessian, coarse, spread_y, spread_z, out, wide):
    rows = hessian.shape[2]
    block = jnp.dot(spread_y[...], coarse[0], precision=HIGH, preferred_element_type=jnp.float32)
    block = jnp.dot(block, spread_z[...], precision=HIGH, preferred_element_type=jnp.float32)
    wide[...] = block.reshape(PART // 4, rows, LANES)

    def fold(k, carry):
        add = wide[k]
        for j in range(4):
            out[0, 4 * k + j] = OMEGA * hessian[0, 4 * k + j] + add
        return carry

    lax.fori_loop(0, PART // 4, fold, 0)


def final_pass(hessian, coarse, spread_y, spread_z):
    parts, xlen, rows = hessian.shape[:3]
    block = pl.BlockSpec((1, PART, rows, LANES), lambda c, i: (c, i, 0, 0))
    coarse_rows = PART // 4 * (rows // 4)
    whole = lambda a: pl.BlockSpec(a.shape, lambda c, i: (0, 0))
    return call(
        final_body,
        (parts, xlen // PART),
        [
            block,
            pl.BlockSpec((1, coarse_rows, LANES // 4), lambda c, i: (c, i, 0)),
            whole(spread_y),
            whole(spread_z),
        ],
        block,
        f32(parts, xlen, rows, LANES),
        [pltpu.VMEM((PART // 4, rows, LANES), jnp.float32)],
        2 * hessian.size,
        8 * hessian.size,
    )(hessian, coarse, spread_y, spread_z)


def coarse_spread(restricted):
    both = ("gz", "gy")
    groups_z = lax.axis_size("gz")
    groups_y = lax.axis_size("gy")
    devices = groups_z * groups_y
    cxlen, cylen, czlen = (restricted.shape[1], restricted.shape[2], restricted.shape[3])
    full_y = groups_y * cylen
    full_z = groups_z * czlen
    each = -(-3 * cxlen // devices)
    table_x = cas_table(cxlen)
    table_y = cas_table(full_y)
    table_z = cas_table(full_z)
    coeffs = jnp.einsum("xi,cijk->cxjk", table_x, restricted, precision=HIGH)
    coeffs = coeffs.reshape(3 * cxlen, cylen, czlen)
    coeffs = jnp.pad(coeffs, ((0, each * devices - 3 * cxlen), (0, 0), (0, 0)))
    planes = lax.all_to_all(coeffs, both, 0, 0, tiled=True)
    planes = planes.reshape(groups_z, groups_y, each, cylen, czlen)
    planes = planes.transpose(2, 1, 3, 0, 4).reshape(each, full_y, full_z)
    planes = jnp.einsum("yj,pjk->pyk", table_y, planes, precision=HIGH)
    planes = jnp.einsum("zk,pyk->pyz", table_z, planes, precision=HIGH)
    line_x = jnp.tile(eigen_line(cxlen), -(-each * devices // cxlen))
    line_x = lax.dynamic_slice_in_dim(line_x, lax.axis_index(both) * each, each, 0)
    total = (
        line_x[:, None, None] + eigen_line(full_y)[None, :, None] + eigen_line(full_z)[None, None, :]
    )
    planes = planes / (GAMMA + COARSE_BETA * total * total)
    planes = jnp.einsum("zk,pyk->pyz", table_z, planes, precision=HIGH)
    planes = jnp.einsum("yj,pjk->pyk", table_y, planes, precision=HIGH)
    planes = planes.reshape(each, groups_y, cylen, groups_z, czlen).transpose(3, 1, 0, 2, 4)
    planes = planes.reshape(devices * each, cylen, czlen)
    coeffs = lax.all_to_all(planes, both, 0, 0, tiled=True)[: 3 * cxlen]
    coeffs = coeffs.reshape(3, cxlen, cylen, czlen)
    coeffs = jnp.einsum("xi,cijk->cxjk", table_x, coeffs, precision=HIGH)
    return coeffs / float(cxlen * full_y * full_z)


def slab_curve(row, inward, left, right):
    lane = lax.broadcasted_iota(jnp.int32, row.shape, 2)
    before = jnp.where(lane == 0, left[:, :, None], jnp.roll(row, 1, 2))
    after = jnp.where(lane == LANES - 1, right[:, :, None], jnp.roll(row, -1, 2))
    near = jnp.roll(row, 1, 1) + jnp.roll(row, -1, 1) + before + after
    return inward - 12.0 * row + 2.0 * near


def lane_curve(left, right):
    spot = lax.broadcasted_iota(jnp.int32, left.shape, 2) % GROUP
    rims = jnp.where(spot < 2, left, right)
    rows = rims.shape[1]
    empty = jnp.zeros_like(rims[:, :1])
    up = jnp.concatenate([rims[:, 1:], empty], axis=1)
    down = jnp.concatenate([empty, rims[:, : rows - 1]], axis=1)
    bent = -2.0 * (
        6.0 * rims - jnp.roll(rims, GROUP, 2) - jnp.roll(rims, -GROUP, 2) - up - down
    )
    plain = jnp.where(spot < 2, jnp.roll(rims, -2, 2), jnp.roll(rims, 2, 2))
    curve = jnp.where(spot == 1, jnp.roll(bent, -1, 2), jnp.roll(bent, 1, 2))
    return BETA * (plain + jnp.where((spot == 1) | (spot == 2), curve, 0.0))


def per_device(velocity, increment, template, deformed):
    xlen, rows = template.shape[0], template.shape[1]

    packed, low0, low1, high0, high1 = state_rims(template, deformed)
    left = shifted(packed, "gz", 1)
    right = shifted(packed, "gz", -1)
    below = shifted(jnp.stack([high0, high1]), "gy", 1)
    above = shifted(jnp.stack([low0, low1]), "gy", -1)
    slabs = (below[0], below[1], above[0], above[1])

    filtered, inc_packed = stencil(increment)

    state, source, s_packed, s_low, s_high = first_state(
        increment, template, deformed, slabs, left, right
    )
    s_left = shifted(s_packed, "gz", 1)
    s_right = shifted(s_packed, "gz", -1)
    s_below = shifted(s_high, "gy", 1)
    s_above = shifted(s_low, "gy", -1)

    inc_left = shifted(inc_packed, "gz", 1)
    inc_right = shifted(inc_packed, "gz", -1)
    edge_lanes = lane_curve(inc_left, inc_right)
    from_left = inc_left.reshape(3, rows, xlen, GROUP)
    from_right = inc_right.reshape(3, rows, xlen, GROUP)
    first_row, last_row = increment[:, :, 0], increment[:, :, rows - 1]
    low_curve = slab_curve(first_row, increment[:, :, 1], from_left[:, 0, :, 1], from_right[:, 0, :, 2])
    high_curve = slab_curve(
        last_row, increment[:, :, rows - 2], from_left[:, rows - 1, :, 1], from_right[:, rows - 1, :, 2]
    )
    from_below = shifted(jnp.stack([high_curve, last_row], axis=2), "gy", 1)
    from_above = shifted(jnp.stack([first_row, low_curve], axis=2), "gy", -1)
    edge_low = BETA * from_below.reshape(3, 2 * xlen, LANES)
    edge_high = BETA * from_above.reshape(3, 2 * xlen, LANES)

    adjoint, f_packed, f_low, f_high = second_state(
        velocity, source, state, s_below, s_above, s_left, s_right
    )
    f_left = shifted(f_packed, "gz", 1)
    f_right = shifted(f_packed, "gz", -1)
    f_below = shifted(f_high, "gy", 1)
    f_above = shifted(f_low, "gy", -1)

    coarse_x = PART // 4
    fold_y = jnp.repeat(jnp.eye(coarse_x * (rows // 4), dtype=jnp.float32), 4, axis=1)
    fold_z = jnp.repeat(jnp.eye(LANES // 4, dtype=jnp.float32), 4, axis=0)
    hessian, restricted = hessian_pass(
        filtered, velocity, adjoint, template, deformed, slabs, left, right, f_below, f_above,
        f_left, f_right, edge_low, edge_high, edge_lanes, fold_y, fold_z,
    )
    coarse = coarse_spread(restricted.reshape(3, xlen // 4, rows // 4, LANES // 4))
    mixed = coarse.reshape(restricted.shape) - OMEGA * restricted
    return final_pass(hessian, mixed, fold_y.T, fold_z.T)


def solution(mesh):
    placed = (
        P(None, None, "gy", "gz"),
        P(None, None, "gy", "gz"),
        P(None, "gy", "gz"),
        P(None, "gy", "gz"),
    )
    return jax.shard_map(
        per_device, mesh=mesh, in_specs=placed, out_specs=P(None, None, "gy", "gz"), check_vma=False
    )
```

```python
import functools
import math

import jax
import jax.numpy as jnp
import numpy as np
from jax import lax
from jax.experimental import pallas as pl
from jax.experimental.pallas import tpu as pltpu
from jax.sharding import PartitionSpec as P

STEP = 0.5
BETA = 0.02
GAMMA = 0.05
COARSE_BETA = 0.025
OMEGA = 1.0 / (0.05 + 42.0 * 0.02)
HIGH = lax.Precision.HIGHEST

PART = 32
GROUP = 4
LANES = 128
TOP = 8
RUN = 8
BATCH = 32
LONG = 64
WIDE = 128
LARGE = 1 << 20


def shifted(value, axis, by):
    peers = lax.axis_size(axis)
    return lax.ppermute(value, axis, [(i, (i + by) % peers) for i in range(peers)])


def cas_table(count):
    index = np.arange(count)
    angle = (index[:, None] * index[None, :] % count) * (2.0 * math.pi / count)
    return jnp.asarray(np.cos(angle) + np.sin(angle), jnp.float32)


def eigen_line(count):
    return jnp.asarray(2.0 - 2.0 * np.cos(np.arange(count) * (2.0 * math.pi / count)), jnp.float32)


def lane_of(rows):
    return lax.broadcasted_iota(jnp.int32, (rows, LANES), 1)


def turn(value, by):
    return pltpu.roll(value, by % LANES if isinstance(by, int) else by, 1)


def turned_to(value, place):
    return pltpu.roll(value, lax.rem(place, LANES), 1)


def turned_from(value, place):
    return pltpu.roll(value, lax.rem(LANES - lax.rem(place, LANES), LANES), 1)


def z_sides(value, rim, lane):
    before = turn(jnp.where(lane == LANES - 1, rim, value), 1)
    after = turn(jnp.where(lane == 0, rim, value), -1)
    return before, after


def planes_loop(count, body, carry=0, step=RUN):
    def several(k, carry):
        for j in range(step):
            carry = body(k * step + j, carry)
        return carry

    return lax.fori_loop(0, count // step, several, carry)


def y_sides(value, low, high):
    rows = value.shape[0]
    row = lax.broadcasted_iota(jnp.int32, value.shape, 0)
    before = jnp.where(row == 0, low, pltpu.roll(value, 1, 0))
    after = jnp.where(row == rows - 1, high, pltpu.roll(value, rows - 1, 0))
    return before, after


def halves(value):
    large = value.astype(jnp.bfloat16)
    small = (value - large.astype(jnp.float32)).astype(jnp.bfloat16)
    return jnp.concatenate([large, small], axis=1)


def doubled(table):
    return jnp.asarray(np.concatenate([table, table], axis=0), jnp.bfloat16)


def product(left, right):
    return jnp.dot(left, right, preferred_element_type=jnp.float32)


def call(body, grid, streamed, kept, out_streamed, out_kept, scratch, flops, moved, grant=12, reused=None):
    counts = [len(streamed), len(kept), len(out_streamed), len(out_kept)]

    def kernel(*refs):
        groups = []
        for count in counts:
            groups.append(refs[:count])
            refs = refs[count:]

        def step(*blocks):
            body(*blocks[: counts[0]], *groups[1], *blocks[counts[0] :], *groups[3], *refs)

        pltpu.emit_pipeline(
            step,
            grid=grid,
            in_specs=[spec for _, spec in streamed],
            out_specs=[spec for _, spec in out_streamed],
        )(*groups[0], *groups[2])

    def placed(array):
        return pltpu.with_memory_space_constraint(array, pltpu.HBM) if array.size >= LARGE else array

    far = pl.BlockSpec(memory_space=pl.ANY)
    near = pl.BlockSpec(memory_space=pltpu.VMEM)
    return pl.pallas_call(
        kernel,
        in_specs=[far] * counts[0] + [near] * counts[1],
        out_specs=[far] * counts[2] + [near] * counts[3],
        out_shape=[jax.ShapeDtypeStruct(shape, jnp.float32) for shape, _ in out_streamed]
        + [pltpu.VMEM(shape, jnp.float32) for shape in out_kept],
        scratch_shapes=scratch,
        input_output_aliases={} if reused is None else {counts[0] + reused[0]: counts[2] + reused[1]},
        cost_estimate=pl.CostEstimate(flops=flops, bytes_accessed=moved, transcendentals=0),
        compiler_params=pltpu.CompilerParams(vmem_limit_bytes=grant * 1024 * 1024),
    )(
        *[placed(array) for array, _ in streamed],
        *[pltpu.with_memory_space_constraint(array, pltpu.VMEM) for array in kept],
    )


def state_rims_body(first, second, packed, low, high):
    rows = first.shape[1]
    lane = lane_of(rows)
    owner = lane // GROUP
    spot = lane % GROUP

    def plane(i, edge):
        a = first[i].astype(jnp.float32)
        b = second[i].astype(jnp.float32)
        low[0, pl.ds(i, 1), :] = a[:1]
        low[1, pl.ds(i, 1), :] = b[:1]
        high[0, pl.ds(i, 1), :] = a[rows - 1 :]
        high[1, pl.ds(i, 1), :] = b[rows - 1 :]
        both = jnp.where(spot < 2, turned_to(a, GROUP * i + 1), turned_to(b, GROUP * i + 3))
        return jnp.where(owner == i, both, edge)

    packed[...] = planes_loop(PART, plane, jnp.zeros((rows, LANES), jnp.float32), 16)


def state_rims(first, second):
    xlen, rows = first.shape[0], first.shape[1]
    block = pl.BlockSpec((PART, rows, LANES), lambda i: (i, 0, 0))
    slab = pl.BlockSpec((2, PART, LANES), lambda i: (0, i, 0))
    return call(
        state_rims_body,
        (xlen // PART,),
        [(first, block), (second, block)],
        [],
        [
            ((rows, GROUP * xlen), pl.BlockSpec((rows, LANES), lambda i: (0, i))),
            ((2, xlen, LANES), slab),
            ((2, xlen, LANES), slab),
        ],
        [],
        [],
        8 * first.size,
        4 * first.size,
    )


def stencil_table():
    cell = np.arange(LANES)
    gap = np.abs(cell[:, None] - cell[None, :])
    outer = np.where(gap == 0, 38.0, np.where(gap == 1, -12.0, np.where(gap == 2, 1.0, 0.0)))
    inner = np.where(gap == 0, -12.0, np.where(gap == 1, 2.0, 0.0))
    table = np.concatenate([outer, inner], axis=1)
    return doubled(table)


def stencil_body(
    before, cells, after, table, packed, low, high, low_curve, high_curve, out, padded, inner
):
    rows = cells.shape[2]
    comp = pl.program_id(0)
    base = pl.program_id(1) * LONG
    owner = lane_of(rows) // GROUP
    here = pl.ds(TOP, rows)

    @pl.when((comp == 0) & (base == 0))
    def _():
        padded[...] = jnp.zeros_like(padded)

    for j in range(2):
        padded[j, here] = before[0, j]
        padded[LONG + 2 + j, here] = after[0, j]

    def fill(i, carry):
        padded[i + 2, here] = cells[0, i]
        return carry

    planes_loop(LONG, fill)

    def middle(j, count):
        flat = padded[pl.ds(j, count), here].reshape(count * rows, LANES)
        both = product(halves(flat), table[...])
        found = []
        for k in range(count):
            value = padded[j + k, here]
            part = both[k * rows : (k + 1) * rows]
            along = padded[j + k - 1, here] + padded[j + k + 1, here]
            core = (
                part[:, LANES:]
                + along
                + (padded[j + k, pl.ds(TOP - 1, rows)] + padded[j + k, pl.ds(TOP + 1, rows)])
            )
            inner[j + k - 1, here] = core
            inner[j + k - 1, TOP - 1 : TOP] = value[:1]
            inner[j + k - 1, TOP + rows : TOP + rows + 1] = value[rows - 1 :]
            found.append((value, part[:, :LANES], core, along))
        return found

    middle(1, 1)
    middle(LONG + 2, 1)

    for b in range(LONG // PART):

        def several(k, edge):
            first = b * PART + k * BATCH
            for j, (value, outer, core, along) in enumerate(middle(first + 2, BATCH)):
                i = first + j
                out[comp, base + i] = GAMMA * value + BETA * outer
                low[0, pl.ds(i, 1), :] = value[:1]
                high[0, pl.ds(i, 1), :] = value[rows - 1 :]
                low_curve[0, pl.ds(i, 1), :] = core[:1] + along[:1]
                high_curve[0, pl.ds(i, 1), :] = core[rows - 1 :] + along[rows - 1 :]
                part = k * BATCH + j
                edge = jnp.where(owner == part, turned_to(value, GROUP * part + 2), edge)
            return edge

        packed[0, :, b * LANES : (b + 1) * LANES] = lax.fori_loop(
            0, PART // BATCH, several, jnp.zeros((rows, LANES), jnp.float32)
        )

    def finish(i, carry):
        around = (inner[i, here] + inner[i + 2, here]) + (
            inner[i + 1, pl.ds(TOP - 1, rows)] + inner[i + 1, pl.ds(TOP + 1, rows)]
        )
        out[comp, base + i] = out[comp, base + i] + BETA * around
        return carry

    planes_loop(LONG, finish)


def stencil(increment, table):
    parts, xlen, rows = increment.shape[:3]
    half = LONG // 2
    pairs = xlen // 2
    slab = pl.BlockSpec((1, LONG, LANES), lambda c, i: (c, i, 0))
    return call(
        stencil_body,
        (parts, xlen // LONG),
        [
            (
                increment,
                pl.BlockSpec(
                    (1, 2, rows, LANES),
                    lambda c, i: (c, lax.rem(half * i + pairs - 1, pairs), 0, 0),
                ),
            ),
            (increment, pl.BlockSpec((1, LONG, rows, LANES), lambda c, i: (c, i, 0, 0))),
            (
                increment,
                pl.BlockSpec(
                    (1, 2, rows, LANES), lambda c, i: (c, lax.rem(half * i + half, pairs), 0, 0)
                ),
            ),
        ],
        [table],
        [
            (
                (parts, rows, GROUP * xlen),
                pl.BlockSpec((1, rows, LONG // PART * LANES), lambda c, i: (c, 0, i)),
            ),
        ]
        + [((parts, xlen, LANES), slab)] * 4,
        [increment.shape],
        [
            pltpu.VMEM((LONG + 4, rows + 2 * TOP, LANES), jnp.float32),
            pltpu.VMEM((LONG + 2, rows + 2 * TOP, LANES), jnp.float32),
        ],
        24 * increment.size,
        4 * increment.size,
        12,
    )


def corner_table():
    table = np.zeros((LANES, LANES))
    table[1::GROUP, 0] = 2.0
    table[2::GROUP, LANES - 1] = 2.0
    return table


def corner_body(low, high, left, right, table, out_low, out_high):
    parts, xlen = low.shape[:2]
    rows = left.shape[1]
    row = lax.broadcasted_iota(jnp.int32, (PART, LANES), 0)
    lane = lax.broadcasted_iota(jnp.int32, (PART, LANES), 1)
    mine = lane // GROUP == row
    for c in range(parts):
        for b in range(xlen // PART):
            planes = slice(b * PART, (b + 1) * PART)
            lanes = slice(b * LANES, (b + 1) * LANES)
            for curve, out, at in ((low, out_low, 0), (high, out_high, rows - 1)):
                rim = jnp.where(
                    lane % GROUP == 1, left[c, at : at + 1, lanes], right[c, at : at + 1, lanes]
                )
                rim = halves(jnp.where(mine, rim, 0.0))
                out[c, planes] = BETA * (curve[c, planes] + product(rim, table[...]))


def corners(low, high, left, right):
    near = pl.BlockSpec(memory_space=pltpu.VMEM)
    return pl.pallas_call(
        corner_body,
        in_specs=[near] * 5,
        out_specs=[near] * 2,
        out_shape=[jax.ShapeDtypeStruct(low.shape, jnp.float32)] * 2,
        cost_estimate=pl.CostEstimate(
            flops=8 * low.size, bytes_accessed=16 * low.size, transcendentals=0
        ),
        compiler_params=pltpu.CompilerParams(vmem_limit_bytes=12 * 1024 * 1024),
    )(low, high, left, right, doubled(corner_table()))


def edges_body(
    low, high, low_curve, high_curve, lanes, filtered, out,
):
    rows = filtered.shape[2]
    base = pl.program_id(0) * PART
    lane = lane_of(rows)
    row = lax.broadcasted_iota(jnp.int32, (8, LANES), 0)
    outer = (lane < 2) | (lane >= LANES - 2)
    for d in range(3):

        def plane(i, carry):
            at = pl.ds(i, 1)
            cyclic = turned_from(lanes[d], GROUP * i + 2)
            value = filtered[d, base + i] + jnp.where(outer, cyclic, 0.0)
            first = jnp.where(row == 1, BETA * low[d, at], 0.0)
            first = jnp.where(row == 0, low_curve[d, at], first)
            last = jnp.where(row == 6, BETA * high[d, at], 0.0)
            last = jnp.where(row == 7, high_curve[d, at], last)
            if rows == 8:
                out[d, base + i] = value + first + last
            else:
                out[d, base + i, :8] = value[:8] + first
                out[d, base + i, 8 : rows - 8] = value[8 : rows - 8]
                out[d, base + i, rows - 8 :] = value[rows - 8 :] + last
            return carry

        planes_loop(PART, plane, 0, 16)


def edges_pass(filtered, low, high, low_curve, high_curve, lanes):
    parts, xlen, rows = filtered.shape[:3]
    slab = pl.BlockSpec((parts, PART, LANES), lambda i: (0, i, 0))
    return call(
        edges_body,
        (xlen // PART,),
        [(low, slab), (high, slab), (low_curve, slab), (high_curve, slab)]
        + [(lanes, pl.BlockSpec((parts, rows, LANES), lambda i: (0, 0, i)))],
        [filtered],
        [],
        [filtered.shape],
        [],
        4 * filtered.size,
        filtered.size,
        4,
        (0, 0),
    )[0]


def gradient_table():
    cell = np.arange(LANES)
    gap = cell[None, :] - cell[:, None]
    slope = (gap == -1).astype(np.float64) - (gap == 1)
    none = np.zeros_like(slope)
    rims = np.zeros((LANES, 2 * LANES))
    rims[0::GROUP, 0] = -1.0
    rims[1::GROUP, LANES - 1] = 1.0
    rims[2::GROUP, LANES] = -1.0
    rims[3::GROUP, 2 * LANES - 1] = 1.0
    return jnp.asarray(np.block([[slope, none], [none, slope], [rims]]), jnp.bfloat16)


def load_states(m0, m0b, m0a, m1, m1b, m1a, lows, highs, rims, table, pad0, pad1, slopes):
    rows = m0.shape[1]
    base = pl.program_id(0) * PART
    here = pl.ds(TOP, rows)
    owner = lane_of(rows) // GROUP
    for which, (ref, before, after, pad) in enumerate(((m0, m0b, m0a, pad0), (m1, m1b, m1a, pad1))):

        @pl.when(base == 0)
        def _():
            pad[0, here] = before[0].astype(jnp.float32)

        pad[base + PART + 1, here] = after[0].astype(jnp.float32)

        def fill(i, carry):
            pad[base + i + 1, here] = ref[i].astype(jnp.float32)
            pad[base + i + 1, pl.ds(TOP - 1, 1)] = lows[which, pl.ds(i, 1), :]
            pad[base + i + 1, pl.ds(TOP + rows, 1)] = highs[which, pl.ds(i, 1), :]
            return carry

        planes_loop(PART, fill)

    def several(k, carry):
        first = k * BATCH
        flat = [
            pad[pl.ds(base + first + 1, BATCH), here].reshape(BATCH * rows, LANES).astype(jnp.bfloat16)
            for pad in (pad0, pad1)
        ]
        edge = jnp.concatenate([jnp.where(owner == first + j, rims, 0.0) for j in range(BATCH)], axis=0)
        both = product(jnp.concatenate(flat + [edge.astype(jnp.bfloat16)], axis=1), table[...])
        slopes[pl.ds(base + first, BATCH)] = both.reshape(BATCH, rows, 2 * LANES)
        return carry

    lax.fori_loop(0, PART // BATCH, several, 0)


def gradients(pad, slope, i, rows):
    here = pl.ds(TOP, rows)
    return (
        pad[i + 2, here] - pad[i, here],
        pad[i + 1, pl.ds(TOP + 1, rows)] - pad[i + 1, pl.ds(TOP - 1, rows)],
        slope,
    )


def merged_rims(left, right, rows):
    spot = lane_of(rows) % GROUP
    return jnp.where(spot % 2 == 0, left[...], right[...])


def first_state_body(
    increment, m0, m0b, m0a, m1, m1b, m1a, lows, highs, left, right, table,
    packed, low, high, state, source, pad0, pad1, slopes,
):
    rows = m0.shape[1]
    base = pl.program_id(0) * PART
    owner = lane_of(rows) // GROUP
    rims = merged_rims(left, right, rows)
    load_states(m0, m0b, m0a, m1, m1b, m1a, lows, highs, rims, table, pad0, pad1, slopes)

    def plane(i, edge):
        g0 = gradients(pad0, slopes[base + i, :, :LANES], base + i, rows)
        g1 = gradients(pad1, slopes[base + i, :, LANES:], base + i, rows)
        u = [increment[d, i] for d in range(3)]
        one = (-0.5 * STEP) * (u[0] * g0[0] + u[1] * g0[1] + u[2] * g0[2])
        state[base + i] = one
        source[base + i] = (0.5 * STEP) * (u[0] * g1[0] + u[1] * g1[1] + u[2] * g1[2])
        low[pl.ds(i, 1), :] = one[:1]
        high[pl.ds(i, 1), :] = one[rows - 1 :]
        return jnp.where(owner == i, turned_to(one, GROUP * i + 1), edge)

    packed[...] = planes_loop(PART, plane, jnp.zeros((rows, LANES), jnp.float32), 16)


def around(array):
    xlen, rows = array.shape[:2]
    return [
        (array, pl.BlockSpec((PART, rows, LANES), lambda i: (i, 0, 0))),
        (array, pl.BlockSpec((1, rows, LANES), lambda i: (lax.rem(PART * i + xlen - 1, xlen), 0, 0))),
        (array, pl.BlockSpec((1, rows, LANES), lambda i: (lax.rem(PART * i + PART, xlen), 0, 0))),
    ]


def first_state(increment, first, second, lows, highs, left, right):
    xlen, rows = first.shape[0], first.shape[1]
    triple = pl.BlockSpec((3, PART, rows, LANES), lambda i: (0, i, 0, 0))
    slab = pl.BlockSpec((PART, LANES), lambda i: (i, 0))
    double = pl.BlockSpec((2, PART, LANES), lambda i: (0, i, 0))
    rim = pl.BlockSpec((rows, LANES), lambda i: (0, i))
    return call(
        first_state_body,
        (xlen // PART,),
        [(increment, triple)]
        + around(first)
        + around(second)
        + [(lows, double), (highs, double), (left, rim), (right, rim)],
        [gradient_table()],
        [((rows, GROUP * xlen), rim), ((xlen, LANES), slab), ((xlen, LANES), slab)],
        [first.shape, first.shape]
        + [(xlen + 2, rows + 2 * TOP, LANES)] * 2
        + [(xlen, rows, 2 * LANES)],
        [],
        24 * first.size,
        16 * first.size,
        6,
    )


def second_state_body(
    velocity, low, high, left, right, state, source, packed, out_low, out_high, adjoint, across
):
    xlen, rows = state.shape[0], state.shape[1]
    base = pl.program_id(0) * PART
    lane = lane_of(rows)
    owner = lane // GROUP
    rims = merged_rims(left, right, rows)

    def lanes_part(i, carry):
        value = state[base + i]
        speed = velocity[2, i]
        before, after = z_sides(value, turned_from(rims, GROUP * i + 1), lane)
        across[i] = (STEP * speed) * jnp.where(speed > 0.0, value - before, after - value)
        return carry

    planes_loop(PART, lanes_part)

    def plane(i, edge):
        value = state[base + i]
        total = (source[base + i] - value) + across[i]
        sides = [
            (
                state[lax.rem(base + i + xlen - 1, xlen)],
                state[lax.rem(base + i + 1, xlen)],
            ),
            y_sides(value, low[pl.ds(i, 1), :], high[pl.ds(i, 1), :]),
        ]
        for d in range(2):
            speed = velocity[d, i]
            slope = jnp.where(speed > 0.0, value - sides[d][0], sides[d][1] - value)
            total = total + (STEP * speed) * slope
        adjoint[base + i] = total
        along = velocity[1, i]
        out_low[pl.ds(i, 1), :] = jnp.maximum(along[:1], 0.0) * total[:1]
        out_high[pl.ds(i, 1), :] = jnp.minimum(along[rows - 1 :], 0.0) * total[rows - 1 :]
        along = velocity[2, i]
        flow = total * jnp.where(
            lane == LANES - 1, jnp.minimum(along, 0.0), jnp.maximum(along, 0.0)
        )
        return jnp.where(owner == i, turned_to(flow, GROUP * i + 1), edge)

    packed[...] = planes_loop(PART, plane, jnp.zeros((rows, LANES), jnp.float32), 16)


def second_state(velocity, source, state, low, high, left, right):
    xlen, rows = state.shape[0], state.shape[1]
    triple = pl.BlockSpec((3, PART, rows, LANES), lambda i: (0, i, 0, 0))
    slab = pl.BlockSpec((PART, LANES), lambda i: (i, 0))
    rim = pl.BlockSpec((rows, LANES), lambda i: (0, i))
    return call(
        second_state_body,
        (xlen // PART,),
        [(velocity, triple), (low, slab), (high, slab), (left, rim), (right, rim)],
        [state, source],
        [((rows, GROUP * xlen), rim), ((xlen, LANES), slab), ((xlen, LANES), slab)],
        [state.shape],
        [pltpu.VMEM((PART, rows, LANES), jnp.float32)],
        30 * state.size,
        12 * state.size,
        6,
        (1, 0),
    )


def fold_table(count):
    return np.repeat(np.eye(count), 4, axis=1)


def hessian_body(
    velocity, speed_b, speed_a, flow_low, flow_high, flow_left, flow_right,
    filtered, adjoint, pad0, pad1, slopes, fold_z, out, restricted, flows, sums, few,
):
    xlen, rows = adjoint.shape[0], adjoint.shape[1]
    base = pl.program_id(0) * PART
    lane = lane_of(rows)
    row = lax.broadcasted_iota(jnp.int32, (rows, LANES), 0)
    ends = merged_rims(flow_left, flow_right, rows)

    def across(i, carry):
        value = adjoint[base + i]
        speed = velocity[2, i]
        rim = turned_from(ends, GROUP * i + 1)
        flows[i] = turn(jnp.where(lane == 0, rim, jnp.maximum(speed, 0.0) * value), -1) - turn(
            jnp.where(lane == LANES - 1, rim, jnp.minimum(speed, 0.0) * value), 1
        )
        return carry

    planes_loop(PART, across)

    def plane(i, carry):
        g0 = gradients(pad0, slopes[base + i, :, :LANES], base + i, rows)
        g1 = gradients(pad1, slopes[base + i, :, LANES:], base + i, rows)
        value = adjoint[base + i]
        sx, sy, sz = (velocity[d, i] for d in range(3))
        before, after = jnp.maximum(i - 1, 0), jnp.minimum(i + 1, PART - 1)
        speed_before = jnp.where(i == 0, speed_b[0, 0], velocity[0, before])
        speed_after = jnp.where(i == PART - 1, speed_a[0, 0], velocity[0, after])
        prev = jnp.minimum(speed_before, 0.0) * adjoint[lax.rem(base + i + xlen - 1, xlen)]
        later = jnp.maximum(speed_after, 0.0) * adjoint[lax.rem(base + i + 1, xlen)]
        inflow = pltpu.roll(jnp.minimum(sy, 0.0) * value, 1, 0)
        outflow = pltpu.roll(jnp.maximum(sy, 0.0) * value, rows - 1, 0)
        change = (
            (later - prev)
            + flows[i]
            + jnp.where(row == rows - 1, flow_high[pl.ds(i, 1), :], outflow)
            - jnp.where(row == 0, flow_low[pl.ds(i, 1), :], inflow)
            - (jnp.abs(sx) + jnp.abs(sy) + jnp.abs(sz)) * value
        )
        half_two = (0.5 * STEP) * value
        half_one = half_two + (0.5 * STEP * STEP) * change
        for d in range(3):
            out[d, i] = filtered[d, base + i] + half_one * g0[d] + half_two * g1[d]
        return carry

    planes_loop(PART, plane)

    count = PART // 4 * (rows // 4)
    for d in range(3):

        def fold(k, carry):
            total = (out[d, 4 * k] + out[d, 4 * k + 1]) + (out[d, 4 * k + 2] + out[d, 4 * k + 3])
            total = total + pltpu.roll(total, rows - 1, 0)
            sums[pl.ds(k * rows, rows)] = total + pltpu.roll(total, rows - 2, 0)
            return carry

        planes_loop(PART // 4, fold)
        few[pl.ds(d * count, count)] = sums[pl.ds(0, count, stride=4)]
    found = product(halves(few[...]), fold_z[...]) * (1.0 / 64.0)
    restricted[...] = found.reshape(3, count, LANES // 4)


def hessian_pass(
    filtered, velocity, adjoint, pads, flow_low, flow_high, flow_left, flow_right,
):
    xlen, rows = adjoint.shape[0], adjoint.shape[1]
    triple = pl.BlockSpec((3, PART, rows, LANES), lambda i: (0, i, 0, 0))
    slab = pl.BlockSpec((PART, LANES), lambda i: (i, 0))
    rim = pl.BlockSpec((rows, LANES), lambda i: (0, i))
    speed_b = pl.BlockSpec(
        (1, 1, rows, LANES), lambda i: (0, lax.rem(PART * i + xlen - 1, xlen), 0, 0)
    )
    speed_a = pl.BlockSpec((1, 1, rows, LANES), lambda i: (0, lax.rem(PART * i + PART, xlen), 0, 0))
    coarse_rows = PART // 4 * (rows // 4)
    return call(
        hessian_body,
        (xlen // PART,),
        [(velocity, triple), (velocity, speed_b), (velocity, speed_a)]
        + [(flow_low, slab), (flow_high, slab), (flow_left, rim), (flow_right, rim)],
        [filtered, adjoint, *pads, doubled(fold_table(LANES // 4).T)],
        [
            (filtered.shape, triple),
            (
                (3, xlen // 4 * (rows // 4), LANES // 4),
                pl.BlockSpec((3, coarse_rows, LANES // 4), lambda i: (0, i, 0)),
            ),
        ],
        [],
        [
            pltpu.VMEM((PART, rows, LANES), jnp.float32),
            pltpu.VMEM((PART // 4 * rows, LANES), jnp.float32),
            pltpu.VMEM((3 * coarse_rows, LANES), jnp.float32),
        ],
        70 * adjoint.size,
        24 * adjoint.size,
        9,
    )


def final_body(coarse, hessian, spread_z, out, wide):
    rows = hessian.shape[2]
    few = rows // 4
    wide[...] = product(halves(coarse[0]), spread_z[...])
    half = lax.broadcasted_iota(jnp.int32, (8, LANES), 0) < 4

    def fold(k, carry):
        add = [
            jnp.where(
                half, wide[pl.ds(k * few + 2 * r, 1), :], wide[pl.ds(k * few + 2 * r + 1, 1), :]
            )
            for r in range(rows // 8)
        ]
        add = jnp.concatenate(add, axis=0)
        for j in range(4):
            out[0, 4 * k + j] = OMEGA * hessian[0, 4 * k + j] + add
        return carry

    planes_loop(WIDE // 4, fold, 0, 2)


def final_pass(hessian, coarse):
    parts, xlen, rows = hessian.shape[:3]
    block = pl.BlockSpec((1, WIDE, rows, LANES), lambda c, i: (c, i, 0, 0))
    coarse_rows = WIDE // 4 * (rows // 4)
    return call(
        final_body,
        (parts, xlen // WIDE),
        [
            (coarse, pl.BlockSpec((1, coarse_rows, LANES // 4), lambda c, i: (c, i, 0))),
            (hessian, block),
        ],
        [doubled(fold_table(LANES // 4))],
        [(hessian.shape, block)],
        [],
        [pltpu.VMEM((coarse_rows, LANES), jnp.float32)],
        2 * hessian.size,
        8 * hessian.size,
        20,
    )[0]


def coarse_spread(restricted):
    both = ("gz", "gy")
    groups_z = lax.axis_size("gz")
    groups_y = lax.axis_size("gy")
    devices = groups_z * groups_y
    cxlen, cylen, czlen = (restricted.shape[1], restricted.shape[2], restricted.shape[3])
    full_y = groups_y * cylen
    full_z = groups_z * czlen
    each = -(-3 * cxlen // devices)
    table_x = cas_table(cxlen)
    table_y = cas_table(full_y)
    table_z = cas_table(full_z)
    coeffs = jnp.einsum("xi,cijk->cxjk", table_x, restricted, precision=HIGH)
    coeffs = coeffs.reshape(3 * cxlen, cylen, czlen)
    coeffs = jnp.pad(coeffs, ((0, each * devices - 3 * cxlen), (0, 0), (0, 0)))
    planes = lax.all_to_all(coeffs, both, 0, 0, tiled=True)
    planes = planes.reshape(groups_z, groups_y, each, cylen, czlen)
    planes = planes.transpose(2, 1, 3, 0, 4).reshape(each, full_y, full_z)
    planes = jnp.einsum("yj,pjk->pyk", table_y, planes, precision=HIGH)
    planes = jnp.einsum("zk,pyk->pyz", table_z, planes, precision=HIGH)
    line_x = jnp.tile(eigen_line(cxlen), -(-each * devices // cxlen))
    line_x = lax.dynamic_slice_in_dim(line_x, lax.axis_index(both) * each, each, 0)
    total = (
        line_x[:, None, None] + eigen_line(full_y)[None, :, None] + eigen_line(full_z)[None, None, :]
    )
    planes = planes / (GAMMA + COARSE_BETA * total * total)
    planes = jnp.einsum("zk,pyk->pyz", table_z, planes, precision=HIGH)
    planes = jnp.einsum("yj,pjk->pyk", table_y, planes, precision=HIGH)
    planes = planes.reshape(each, groups_y, cylen, groups_z, czlen).transpose(3, 1, 0, 2, 4)
    planes = planes.reshape(devices * each, cylen, czlen)
    coeffs = lax.all_to_all(planes, both, 0, 0, tiled=True)[: 3 * cxlen]
    coeffs = coeffs.reshape(3, cxlen, cylen, czlen)
    coeffs = jnp.einsum("xi,cijk->cxjk", table_x, coeffs, precision=HIGH)
    return coeffs / float(cxlen * full_y * full_z)


def lane_curve(left, right):
    spot = lax.broadcasted_iota(jnp.int32, left.shape, 2) % GROUP
    rims = jnp.where(spot < 2, left, right)
    rows = rims.shape[1]
    empty = jnp.zeros_like(rims[:, :1])
    up = jnp.concatenate([rims[:, 1:], empty], axis=1)
    down = jnp.concatenate([empty, rims[:, : rows - 1]], axis=1)
    bent = -2.0 * (
        6.0 * rims - jnp.roll(rims, GROUP, 2) - jnp.roll(rims, -GROUP, 2) - up - down
    )
    plain = jnp.where(spot < 2, jnp.roll(rims, -2, 2), jnp.roll(rims, 2, 2))
    curve = jnp.where(spot == 1, jnp.roll(bent, -1, 2), jnp.roll(bent, 1, 2))
    return BETA * (plain + jnp.where((spot == 1) | (spot == 2), curve, 0.0))


def per_device(velocity, increment, template, deformed):
    xlen, rows = template.shape[0], template.shape[1]

    packed, low, high = state_rims(template, deformed)
    packed, low, high, table = lax.optimization_barrier((packed, low, high, stencil_table()))
    left = shifted(packed, "gz", 1)
    right = shifted(packed, "gz", -1)
    lows = shifted(high, "gy", 1)
    highs = shifted(low, "gy", -1)

    inc_packed, inc_low, inc_high, low_curve, high_curve, filtered = stencil(increment, table)
    inc_packed, inc_low, inc_high, left, right, lows, highs = lax.optimization_barrier(
        (inc_packed, inc_low, inc_high, left, right, lows, highs)
    )
    inc_left = shifted(inc_packed, "gz", 1)
    inc_right = shifted(inc_packed, "gz", -1)
    inc_lows = shifted(inc_high, "gy", 1)
    inc_highs = shifted(inc_low, "gy", -1)

    s_packed, s_low, s_high, state, source, *pads = first_state(
        increment, template, deformed, lows, highs, left, right
    )
    s_left = shifted(s_packed, "gz", 1)
    s_right = shifted(s_packed, "gz", -1)
    s_below = shifted(s_high, "gy", 1)
    s_above = shifted(s_low, "gy", -1)

    low_curve, high_curve = corners(low_curve, high_curve, inc_left, inc_right)
    s_left, low_curve, high_curve = lax.optimization_barrier((s_left, low_curve, high_curve))
    low_curves = shifted(high_curve, "gy", 1)
    high_curves = shifted(low_curve, "gy", -1)

    f_packed, f_low, f_high, adjoint = second_state(
        velocity, source, state, s_below, s_above, s_left, s_right
    )
    f_packed, f_low, f_high, low_curves, high_curves = lax.optimization_barrier(
        (f_packed, f_low, f_high, low_curves, high_curves)
    )
    f_left = shifted(f_packed, "gz", 1)
    f_right = shifted(f_packed, "gz", -1)
    f_below = shifted(f_high, "gy", 1)
    f_above = shifted(f_low, "gy", -1)

    filtered = edges_pass(
        filtered, inc_lows, inc_highs, low_curves, high_curves, lane_curve(inc_left, inc_right)
    )
    hessian, restricted = hessian_pass(
        filtered, velocity, adjoint, pads, f_below, f_above, f_left, f_right
    )
    coarse = coarse_spread(restricted.reshape(3, xlen // 4, rows // 4, LANES // 4))
    mixed = coarse.reshape(restricted.shape) - OMEGA * restricted
    return final_pass(hessian, mixed)


def solution(mesh):
    placed = (
        P(None, None, "gy", "gz"),
        P(None, None, "gy", "gz"),
        P(None, "gy", "gz"),
        P(None, "gy", "gz"),
    )
    return jax.shard_map(
        per_device, mesh=mesh, in_specs=placed, out_specs=P(None, None, "gy", "gz"), check_vma=False
    )
```

```python
import functools
import math

import jax
import jax.numpy as jnp
import numpy as np
from jax import lax
from jax.experimental import pallas as pl
from jax.experimental.pallas import tpu as pltpu
from jax.sharding import PartitionSpec as P

STEP = 0.5
BETA = 0.02
GAMMA = 0.05
COARSE_BETA = 0.025
OMEGA = 1.0 / (0.05 + 42.0 * 0.02)
HIGH = lax.Precision.HIGHEST

PART = 32
GROUP = 4
LANES = 128
TOP = 8
RUN = 8
BATCH = 32
LONG = 64
WIDE = 128
LARGE = 1 << 20


def shifted(value, axis, by):
    peers = lax.axis_size(axis)
    return lax.ppermute(value, axis, [(i, (i + by) % peers) for i in range(peers)])


def cas_table(count):
    index = np.arange(count)
    angle = (index[:, None] * index[None, :] % count) * (2.0 * math.pi / count)
    return jnp.asarray(np.cos(angle) + np.sin(angle), jnp.float32)


def eigen_line(count):
    return jnp.asarray(2.0 - 2.0 * np.cos(np.arange(count) * (2.0 * math.pi / count)), jnp.float32)


def lane_of(rows):
    return lax.broadcasted_iota(jnp.int32, (rows, LANES), 1)


def turn(value, by):
    return pltpu.roll(value, by % LANES if isinstance(by, int) else by, 1)


def turned_to(value, place):
    return pltpu.roll(value, lax.rem(place, LANES), 1)


def turned_from(value, place):
    return pltpu.roll(value, lax.rem(LANES - lax.rem(place, LANES), LANES), 1)


def z_sides(value, rim, lane):
    before = jnp.where(lane == 0, rim, turn(value, 1))
    after = jnp.where(lane == LANES - 1, rim, turn(value, -1))
    return before, after


def planes_loop(count, body, carry=0, step=RUN):
    def several(k, carry):
        for j in range(step):
            carry = body(k * step + j, carry)
        return carry

    return lax.fori_loop(0, count // step, several, carry)


def y_sides(value, low, high):
    rows = value.shape[0]
    row = lax.broadcasted_iota(jnp.int32, value.shape, 0)
    before = jnp.where(row == 0, low, pltpu.roll(value, 1, 0))
    after = jnp.where(row == rows - 1, high, pltpu.roll(value, rows - 1, 0))
    return before, after


def halves(value):
    large = value.astype(jnp.bfloat16)
    small = (value - large.astype(jnp.float32)).astype(jnp.bfloat16)
    return jnp.concatenate([large, small], axis=1)


def doubled(table):
    return jnp.asarray(np.concatenate([table, table], axis=0), jnp.bfloat16)


def product(left, right):
    return jnp.dot(left, right, preferred_element_type=jnp.float32)


def call(body, grid, streamed, kept, out_streamed, out_kept, scratch, flops, moved, grant=12, reused=None):
    counts = [len(streamed), len(kept), len(out_streamed), len(out_kept)]

    def kernel(*refs):
        groups = []
        for count in counts:
            groups.append(refs[:count])
            refs = refs[count:]

        def step(*blocks):
            body(*blocks[: counts[0]], *groups[1], *blocks[counts[0] :], *groups[3], *refs)

        pltpu.emit_pipeline(
            step,
            grid=grid,
            in_specs=[spec for _, spec in streamed],
            out_specs=[spec for _, spec in out_streamed],
        )(*groups[0], *groups[2])

    def placed(array):
        return pltpu.with_memory_space_constraint(array, pltpu.HBM) if array.size >= LARGE else array

    far = pl.BlockSpec(memory_space=pl.ANY)
    near = pl.BlockSpec(memory_space=pltpu.VMEM)
    return pl.pallas_call(
        kernel,
        in_specs=[far] * counts[0] + [near] * counts[1],
        out_specs=[far] * counts[2] + [near] * counts[3],
        out_shape=[jax.ShapeDtypeStruct(shape, jnp.float32) for shape, _ in out_streamed]
        + [pltpu.VMEM(shape, jnp.float32) for shape in out_kept],
        scratch_shapes=scratch,
        input_output_aliases={} if reused is None else {counts[0] + reused[0]: counts[2] + reused[1]},
        cost_estimate=pl.CostEstimate(flops=flops, bytes_accessed=moved, transcendentals=0),
        compiler_params=pltpu.CompilerParams(vmem_limit_bytes=grant * 1024 * 1024),
    )(
        *[placed(array) for array, _ in streamed],
        *[pltpu.with_memory_space_constraint(array, pltpu.VMEM) for array in kept],
    )


def state_rims_body(first, second, packed, low, high):
    rows = first.shape[1]
    lane = lane_of(rows)
    owner = lane // GROUP
    spot = lane % GROUP

    def plane(i, edge):
        a = first[i].astype(jnp.float32)
        b = second[i].astype(jnp.float32)
        low[0, pl.ds(i, 1), :] = a[:1]
        low[1, pl.ds(i, 1), :] = b[:1]
        high[0, pl.ds(i, 1), :] = a[rows - 1 :]
        high[1, pl.ds(i, 1), :] = b[rows - 1 :]
        both = jnp.where(spot < 2, turned_to(a, GROUP * i + 1), turned_to(b, GROUP * i + 3))
        return jnp.where(owner == i, both, edge)

    packed[...] = planes_loop(PART, plane, jnp.zeros((rows, LANES), jnp.float32), 32)


def state_rims(first, second):
    xlen, rows = first.shape[0], first.shape[1]
    block = pl.BlockSpec((PART, rows, LANES), lambda i: (i, 0, 0))
    slab = pl.BlockSpec((2, PART, LANES), lambda i: (0, i, 0))
    return call(
        state_rims_body,
        (xlen // PART,),
        [(first, block), (second, block)],
        [],
        [
            ((rows, GROUP * xlen), pl.BlockSpec((rows, LANES), lambda i: (0, i))),
            ((2, xlen, LANES), slab),
            ((2, xlen, LANES), slab),
        ],
        [],
        [],
        8 * first.size,
        4 * first.size,
    )


def stencil_table():
    cell = np.arange(LANES)
    gap = np.abs(cell[:, None] - cell[None, :])
    outer = np.where(gap == 0, 38.0, np.where(gap == 1, -12.0, np.where(gap == 2, 1.0, 0.0)))
    inner = np.where(gap == 0, -12.0, np.where(gap == 1, 2.0, 0.0))
    table = np.concatenate([outer, inner], axis=1)
    return doubled(table)


def stencil_body(
    before, cells, after, table, packed, low, high, low_curve, high_curve, out, padded, inner
):
    rows = cells.shape[2]
    comp = pl.program_id(0)
    base = pl.program_id(1) * LONG
    owner = lane_of(rows) // GROUP
    here = pl.ds(TOP, rows)

    @pl.when((comp == 0) & (base == 0))
    def _():
        padded[...] = jnp.zeros_like(padded)

    for j in range(2):
        padded[j, here] = before[0, j]
        padded[LONG + 2 + j, here] = after[0, j]

    def fill(i, carry):
        padded[i + 2, here] = cells[0, i]
        return carry

    planes_loop(LONG, fill)

    def middle(j, count):
        flat = padded[pl.ds(j, count), here].reshape(count * rows, LANES)
        both = product(halves(flat), table[...])
        found = []
        for k in range(count):
            value = padded[j + k, here]
            part = both[k * rows : (k + 1) * rows]
            along = padded[j + k - 1, here] + padded[j + k + 1, here]
            core = (
                part[:, LANES:]
                + along
                + (padded[j + k, pl.ds(TOP - 1, rows)] + padded[j + k, pl.ds(TOP + 1, rows)])
            )
            inner[j + k - 1, here] = core
            inner[j + k - 1, TOP - 1 : TOP] = value[:1]
            inner[j + k - 1, TOP + rows : TOP + rows + 1] = value[rows - 1 :]
            found.append((value, part[:, :LANES], core, along))
        return found

    middle(1, 1)
    middle(LONG + 2, 1)

    for b in range(LONG // PART):

        def several(k, edge):
            first = b * PART + k * BATCH
            for j, (value, outer, core, along) in enumerate(middle(first + 2, BATCH)):
                i = first + j
                out[comp, base + i] = GAMMA * value + BETA * outer
                low[0, pl.ds(i, 1), :] = value[:1]
                high[0, pl.ds(i, 1), :] = value[rows - 1 :]
                low_curve[0, pl.ds(i, 1), :] = core[:1] + along[:1]
                high_curve[0, pl.ds(i, 1), :] = core[rows - 1 :] + along[rows - 1 :]
                part = k * BATCH + j
                edge = jnp.where(owner == part, turned_to(value, GROUP * part + 2), edge)
            return edge

        packed[0, :, b * LANES : (b + 1) * LANES] = lax.fori_loop(
            0, PART // BATCH, several, jnp.zeros((rows, LANES), jnp.float32)
        )

    def finish(i, carry):
        around = (inner[i, here] + inner[i + 2, here]) + (
            inner[i + 1, pl.ds(TOP - 1, rows)] + inner[i + 1, pl.ds(TOP + 1, rows)]
        )
        out[comp, base + i] = out[comp, base + i] + BETA * around
        return carry

    planes_loop(LONG, finish)


def stencil(increment, table):
    parts, xlen, rows = increment.shape[:3]
    half = LONG // 2
    pairs = xlen // 2
    slab = pl.BlockSpec((1, LONG, LANES), lambda c, i: (c, i, 0))
    return call(
        stencil_body,
        (parts, xlen // LONG),
        [
            (
                increment,
                pl.BlockSpec(
                    (1, 2, rows, LANES),
                    lambda c, i: (c, lax.rem(half * i + pairs - 1, pairs), 0, 0),
                ),
            ),
            (increment, pl.BlockSpec((1, LONG, rows, LANES), lambda c, i: (c, i, 0, 0))),
            (
                increment,
                pl.BlockSpec(
                    (1, 2, rows, LANES), lambda c, i: (c, lax.rem(half * i + half, pairs), 0, 0)
                ),
            ),
        ],
        [table],
        [
            (
                (parts, rows, GROUP * xlen),
                pl.BlockSpec((1, rows, LONG // PART * LANES), lambda c, i: (c, 0, i)),
            ),
        ]
        + [((parts, xlen, LANES), slab)] * 4,
        [increment.shape],
        [
            pltpu.VMEM((LONG + 4, rows + 2 * TOP, LANES), jnp.float32),
            pltpu.VMEM((LONG + 2, rows + 2 * TOP, LANES), jnp.float32),
        ],
        24 * increment.size,
        4 * increment.size,
        12,
    )


def corner_table():
    table = np.zeros((LANES, LANES))
    table[1::GROUP, 0] = 2.0
    table[2::GROUP, LANES - 1] = 2.0
    return table


def corner_body(low, high, left, right, table, out_low, out_high):
    parts, xlen = low.shape[:2]
    rows = left.shape[1]
    row = lax.broadcasted_iota(jnp.int32, (PART, LANES), 0)
    lane = lax.broadcasted_iota(jnp.int32, (PART, LANES), 1)
    mine = lane // GROUP == row
    for c in range(parts):
        for b in range(xlen // PART):
            planes = slice(b * PART, (b + 1) * PART)
            lanes = slice(b * LANES, (b + 1) * LANES)
            for curve, out, at in ((low, out_low, 0), (high, out_high, rows - 1)):
                rim = jnp.where(
                    lane % GROUP == 1, left[c, at : at + 1, lanes], right[c, at : at + 1, lanes]
                )
                rim = halves(jnp.where(mine, rim, 0.0))
                out[c, planes] = BETA * (curve[c, planes] + product(rim, table[...]))


def corners(low, high, left, right):
    near = pl.BlockSpec(memory_space=pltpu.VMEM)
    return pl.pallas_call(
        corner_body,
        in_specs=[near] * 5,
        out_specs=[near] * 2,
        out_shape=[jax.ShapeDtypeStruct(low.shape, jnp.float32)] * 2,
        cost_estimate=pl.CostEstimate(
            flops=8 * low.size, bytes_accessed=16 * low.size, transcendentals=0
        ),
        compiler_params=pltpu.CompilerParams(vmem_limit_bytes=12 * 1024 * 1024),
    )(low, high, left, right, doubled(corner_table()))


def edges_body(
    low, high, low_curve, high_curve, lanes, filtered, out,
):
    rows = filtered.shape[2]
    base = pl.program_id(0) * PART
    lane = lane_of(rows)
    row = lax.broadcasted_iota(jnp.int32, (8, LANES), 0)
    outer = (lane < 2) | (lane >= LANES - 2)
    for d in range(3):

        def plane(i, carry):
            at = pl.ds(i, 1)
            cyclic = turned_from(lanes[d], GROUP * i + 2)
            value = filtered[d, base + i] + jnp.where(outer, cyclic, 0.0)
            first = jnp.where(row == 1, BETA * low[d, at], 0.0)
            first = jnp.where(row == 0, low_curve[d, at], first)
            last = jnp.where(row == 6, BETA * high[d, at], 0.0)
            last = jnp.where(row == 7, high_curve[d, at], last)
            if rows == 8:
                out[d, base + i] = value + first + last
            else:
                out[d, base + i, :8] = value[:8] + first
                out[d, base + i, 8 : rows - 8] = value[8 : rows - 8]
                out[d, base + i, rows - 8 :] = value[rows - 8 :] + last
            return carry

        planes_loop(PART, plane, 0, 32)


def edges_pass(filtered, low, high, low_curve, high_curve, lanes):
    parts, xlen, rows = filtered.shape[:3]
    slab = pl.BlockSpec((parts, PART, LANES), lambda i: (0, i, 0))
    return call(
        edges_body,
        (xlen // PART,),
        [(low, slab), (high, slab), (low_curve, slab), (high_curve, slab)]
        + [(lanes, pl.BlockSpec((parts, rows, LANES), lambda i: (0, 0, i)))],
        [filtered],
        [],
        [filtered.shape],
        [],
        4 * filtered.size,
        filtered.size,
        4,
        (0, 0),
    )[0]


def gradient_table():
    cell = np.arange(LANES)
    gap = cell[None, :] - cell[:, None]
    slope = (gap == -1).astype(np.float64) - (gap == 1)
    none = np.zeros_like(slope)
    rims = np.zeros((LANES, 2 * LANES))
    rims[0::GROUP, 0] = -1.0
    rims[1::GROUP, LANES - 1] = 1.0
    rims[2::GROUP, LANES] = -1.0
    rims[3::GROUP, 2 * LANES - 1] = 1.0
    return jnp.asarray(np.block([[slope, none], [none, slope], [rims]]), jnp.bfloat16)


def load_states(m0, m0b, m0a, m1, m1b, m1a, lows, highs, rims, table, pad0, pad1, slopes):
    rows = m0.shape[1]
    base = pl.program_id(0) * PART
    here = pl.ds(TOP, rows)
    owner = lane_of(rows) // GROUP
    for which, (ref, before, after, pad) in enumerate(((m0, m0b, m0a, pad0), (m1, m1b, m1a, pad1))):

        @pl.when(base == 0)
        def _():
            pad[0, here] = before[0].astype(jnp.float32)

        pad[base + PART + 1, here] = after[0].astype(jnp.float32)

        def fill(i, carry):
            pad[base + i + 1, here] = ref[i].astype(jnp.float32)
            pad[base + i + 1, pl.ds(TOP - 1, 1)] = lows[which, pl.ds(i, 1), :]
            pad[base + i + 1, pl.ds(TOP + rows, 1)] = highs[which, pl.ds(i, 1), :]
            return carry

        planes_loop(PART, fill)

    def several(k, carry):
        first = k * BATCH
        flat = [
            pad[pl.ds(base + first + 1, BATCH), here].reshape(BATCH * rows, LANES).astype(jnp.bfloat16)
            for pad in (pad0, pad1)
        ]
        edge = jnp.concatenate([jnp.where(owner == first + j, rims, 0.0) for j in range(BATCH)], axis=0)
        both = product(jnp.concatenate(flat + [edge.astype(jnp.bfloat16)], axis=1), table[...])
        slopes[pl.ds(base + first, BATCH)] = both.reshape(BATCH, rows, 2 * LANES)
        return carry

    lax.fori_loop(0, PART // BATCH, several, 0)


def gradients(pad, slope, i, rows):
    here = pl.ds(TOP, rows)
    return (
        pad[i + 2, here] - pad[i, here],
        pad[i + 1, pl.ds(TOP + 1, rows)] - pad[i + 1, pl.ds(TOP - 1, rows)],
        slope,
    )


def crossed_rims(left, right, rows):
    rims = merged_rims(left, right, rows)
    return jnp.where(lane_of(rows) % 2 == 0, turn(rims, -1), turn(rims, 1))


def merged_rims(left, right, rows):
    spot = lane_of(rows) % GROUP
    return jnp.where(spot % 2 == 0, left[...], right[...])


def first_state_body(
    increment, m0, m0b, m0a, m1, m1b, m1a, lows, highs, left, right, table,
    packed, low, high, state, source, pad0, pad1, slopes,
):
    rows = m0.shape[1]
    base = pl.program_id(0) * PART
    owner = lane_of(rows) // GROUP
    rims = merged_rims(left, right, rows)
    load_states(m0, m0b, m0a, m1, m1b, m1a, lows, highs, rims, table, pad0, pad1, slopes)

    def plane(i, edge):
        g0 = gradients(pad0, slopes[base + i, :, :LANES], base + i, rows)
        g1 = gradients(pad1, slopes[base + i, :, LANES:], base + i, rows)
        u = [increment[d, i] for d in range(3)]
        one = (-0.5 * STEP) * (u[0] * g0[0] + u[1] * g0[1] + u[2] * g0[2])
        state[base + i] = one
        source[base + i] = (0.5 * STEP) * (u[0] * g1[0] + u[1] * g1[1] + u[2] * g1[2])
        low[pl.ds(i, 1), :] = one[:1]
        high[pl.ds(i, 1), :] = one[rows - 1 :]
        return jnp.where(owner == i, turned_to(one, GROUP * i + 1), edge)

    packed[...] = planes_loop(PART, plane, jnp.zeros((rows, LANES), jnp.float32), 16)


def around(array):
    xlen, rows = array.shape[:2]
    return [
        (array, pl.BlockSpec((PART, rows, LANES), lambda i: (i, 0, 0))),
        (array, pl.BlockSpec((1, rows, LANES), lambda i: (lax.rem(PART * i + xlen - 1, xlen), 0, 0))),
        (array, pl.BlockSpec((1, rows, LANES), lambda i: (lax.rem(PART * i + PART, xlen), 0, 0))),
    ]


def first_state(increment, first, second, lows, highs, left, right):
    xlen, rows = first.shape[0], first.shape[1]
    triple = pl.BlockSpec((3, PART, rows, LANES), lambda i: (0, i, 0, 0))
    slab = pl.BlockSpec((PART, LANES), lambda i: (i, 0))
    double = pl.BlockSpec((2, PART, LANES), lambda i: (0, i, 0))
    rim = pl.BlockSpec((rows, LANES), lambda i: (0, i))
    return call(
        first_state_body,
        (xlen // PART,),
        [(increment, triple)]
        + around(first)
        + around(second)
        + [(lows, double), (highs, double), (left, rim), (right, rim)],
        [gradient_table()],
        [((rows, GROUP * xlen), rim), ((xlen, LANES), slab), ((xlen, LANES), slab)],
        [first.shape, first.shape]
        + [(xlen + 2, rows + 2 * TOP, LANES)] * 2
        + [(xlen, rows, 2 * LANES)],
        [],
        24 * first.size,
        16 * first.size,
        6,
    )


def second_state_body(
    velocity, low, high, left, right, state, source, packed, out_low, out_high, adjoint, across
):
    xlen, rows = state.shape[0], state.shape[1]
    base = pl.program_id(0) * PART
    lane = lane_of(rows)
    owner = lane // GROUP
    rims = crossed_rims(left, right, rows)

    def lanes_part(i, carry):
        value = state[base + i]
        speed = velocity[2, i]
        before, after = z_sides(value, turned_from(rims, GROUP * i + 1), lane)
        across[i] = (STEP * speed) * jnp.where(speed > 0.0, value - before, after - value)
        return carry

    planes_loop(PART, lanes_part, 0, 16)

    def plane(i, edge):
        value = state[base + i]
        total = (source[base + i] - value) + across[i]
        sides = [
            (
                state[lax.rem(base + i + xlen - 1, xlen)],
                state[lax.rem(base + i + 1, xlen)],
            ),
            y_sides(value, low[pl.ds(i, 1), :], high[pl.ds(i, 1), :]),
        ]
        for d in range(2):
            speed = velocity[d, i]
            slope = jnp.where(speed > 0.0, value - sides[d][0], sides[d][1] - value)
            total = total + (STEP * speed) * slope
        adjoint[base + i] = total
        along = velocity[1, i]
        out_low[pl.ds(i, 1), :] = jnp.maximum(along[:1], 0.0) * total[:1]
        out_high[pl.ds(i, 1), :] = jnp.minimum(along[rows - 1 :], 0.0) * total[rows - 1 :]
        along = velocity[2, i]
        flow = total * jnp.where(
            lane == LANES - 1, jnp.minimum(along, 0.0), jnp.maximum(along, 0.0)
        )
        return jnp.where(owner == i, turned_to(flow, GROUP * i + 1), edge)

    packed[...] = planes_loop(PART, plane, jnp.zeros((rows, LANES), jnp.float32), 16)


def second_state(velocity, source, state, low, high, left, right):
    xlen, rows = state.shape[0], state.shape[1]
    triple = pl.BlockSpec((3, PART, rows, LANES), lambda i: (0, i, 0, 0))
    slab = pl.BlockSpec((PART, LANES), lambda i: (i, 0))
    rim = pl.BlockSpec((rows, LANES), lambda i: (0, i))
    return call(
        second_state_body,
        (xlen // PART,),
        [(velocity, triple), (low, slab), (high, slab), (left, rim), (right, rim)],
        [state, source],
        [((rows, GROUP * xlen), rim), ((xlen, LANES), slab), ((xlen, LANES), slab)],
        [state.shape],
        [pltpu.VMEM((PART, rows, LANES), jnp.float32)],
        30 * state.size,
        12 * state.size,
        6,
        (1, 0),
    )


def fold_table(count):
    return np.repeat(np.eye(count), 4, axis=1)


def hessian_body(
    velocity, speed_b, speed_a, flow_low, flow_high, flow_left, flow_right,
    filtered, adjoint, pad0, pad1, slopes, fold_z, out, restricted, flows, sums, few,
):
    xlen, rows = adjoint.shape[0], adjoint.shape[1]
    base = pl.program_id(0) * PART
    lane = lane_of(rows)
    row = lax.broadcasted_iota(jnp.int32, (rows, LANES), 0)
    ends = crossed_rims(flow_left, flow_right, rows)

    def across(i, carry):
        value = adjoint[base + i]
        speed = velocity[2, i]
        rim = turned_from(ends, GROUP * i + 1)
        later = turn(jnp.maximum(speed, 0.0) * value, -1)
        prev = turn(jnp.minimum(speed, 0.0) * value, 1)
        flows[i] = jnp.where(lane == LANES - 1, rim, later) - jnp.where(lane == 0, rim, prev)
        return carry

    planes_loop(PART, across, 0, 16)

    def plane(i, carry):
        g0 = gradients(pad0, slopes[base + i, :, :LANES], base + i, rows)
        g1 = gradients(pad1, slopes[base + i, :, LANES:], base + i, rows)
        value = adjoint[base + i]
        sx, sy, sz = (velocity[d, i] for d in range(3))
        before, after = jnp.maximum(i - 1, 0), jnp.minimum(i + 1, PART - 1)
        speed_before = jnp.where(i == 0, speed_b[0, 0], velocity[0, before])
        speed_after = jnp.where(i == PART - 1, speed_a[0, 0], velocity[0, after])
        prev = jnp.minimum(speed_before, 0.0) * adjoint[lax.rem(base + i + xlen - 1, xlen)]
        later = jnp.maximum(speed_after, 0.0) * adjoint[lax.rem(base + i + 1, xlen)]
        inflow = pltpu.roll(jnp.minimum(sy, 0.0) * value, 1, 0)
        outflow = pltpu.roll(jnp.maximum(sy, 0.0) * value, rows - 1, 0)
        change = (
            (later - prev)
            + flows[i]
            + jnp.where(row == rows - 1, flow_high[pl.ds(i, 1), :], outflow)
            - jnp.where(row == 0, flow_low[pl.ds(i, 1), :], inflow)
            - (jnp.abs(sx) + jnp.abs(sy) + jnp.abs(sz)) * value
        )
        half_two = (0.5 * STEP) * value
        half_one = half_two + (0.5 * STEP * STEP) * change
        for d in range(3):
            out[d, i] = filtered[d, base + i] + half_one * g0[d] + half_two * g1[d]
        return carry

    planes_loop(PART, plane)

    count = PART // 4 * (rows // 4)
    for d in range(3):

        def fold(k, carry):
            total = (out[d, 4 * k] + out[d, 4 * k + 1]) + (out[d, 4 * k + 2] + out[d, 4 * k + 3])
            total = total + pltpu.roll(total, rows - 1, 0)
            sums[pl.ds(k * rows, rows)] = total + pltpu.roll(total, rows - 2, 0)
            return carry

        planes_loop(PART // 4, fold)
        few[pl.ds(d * count, count)] = sums[pl.ds(0, count, stride=4)]
    found = product(halves(few[...]), fold_z[...]) * (1.0 / 64.0)
    restricted[...] = found.reshape(3, count, LANES // 4)


def hessian_pass(
    filtered, velocity, adjoint, pads, flow_low, flow_high, flow_left, flow_right,
):
    xlen, rows = adjoint.shape[0], adjoint.shape[1]
    triple = pl.BlockSpec((3, PART, rows, LANES), lambda i: (0, i, 0, 0))
    slab = pl.BlockSpec((PART, LANES), lambda i: (i, 0))
    rim = pl.BlockSpec((rows, LANES), lambda i: (0, i))
    speed_b = pl.BlockSpec(
        (1, 1, rows, LANES), lambda i: (0, lax.rem(PART * i + xlen - 1, xlen), 0, 0)
    )
    speed_a = pl.BlockSpec((1, 1, rows, LANES), lambda i: (0, lax.rem(PART * i + PART, xlen), 0, 0))
    coarse_rows = PART // 4 * (rows // 4)
    return call(
        hessian_body,
        (xlen // PART,),
        [(velocity, triple), (velocity, speed_b), (velocity, speed_a)]
        + [(flow_low, slab), (flow_high, slab), (flow_left, rim), (flow_right, rim)],
        [filtered, adjoint, *pads, doubled(fold_table(LANES // 4).T)],
        [
            (filtered.shape, triple),
            (
                (3, xlen // 4 * (rows // 4), LANES // 4),
                pl.BlockSpec((3, coarse_rows, LANES // 4), lambda i: (0, i, 0)),
            ),
        ],
        [],
        [
            pltpu.VMEM((PART, rows, LANES), jnp.float32),
            pltpu.VMEM((PART // 4 * rows, LANES), jnp.float32),
            pltpu.VMEM((3 * coarse_rows, LANES), jnp.float32),
        ],
        70 * adjoint.size,
        24 * adjoint.size,
        9,
    )


def final_body(coarse, hessian, spread_z, out, wide):
    rows = hessian.shape[2]
    few = rows // 4
    wide[...] = product(halves(coarse[0]), spread_z[...])
    half = lax.broadcasted_iota(jnp.int32, (8, LANES), 0) < 4

    def fold(k, carry):
        add = [
            jnp.where(
                half, wide[pl.ds(k * few + 2 * r, 1), :], wide[pl.ds(k * few + 2 * r + 1, 1), :]
            )
            for r in range(rows // 8)
        ]
        add = jnp.concatenate(add, axis=0)
        for j in range(4):
            out[0, 4 * k + j] = OMEGA * hessian[0, 4 * k + j] + add
        return carry

    planes_loop(WIDE // 4, fold, 0, 2)


def final_pass(hessian, coarse):
    parts, xlen, rows = hessian.shape[:3]
    block = pl.BlockSpec((1, WIDE, rows, LANES), lambda c, i: (c, i, 0, 0))
    coarse_rows = WIDE // 4 * (rows // 4)
    return call(
        final_body,
        (parts, xlen // WIDE),
        [
            (coarse, pl.BlockSpec((1, coarse_rows, LANES // 4), lambda c, i: (c, i, 0))),
            (hessian, block),
        ],
        [doubled(fold_table(LANES // 4))],
        [(hessian.shape, block)],
        [],
        [pltpu.VMEM((coarse_rows, LANES), jnp.float32)],
        2 * hessian.size,
        8 * hessian.size,
        20,
    )[0]


def coarse_spread(restricted):
    both = ("gz", "gy")
    groups_z = lax.axis_size("gz")
    groups_y = lax.axis_size("gy")
    devices = groups_z * groups_y
    cxlen, cylen, czlen = (restricted.shape[1], restricted.shape[2], restricted.shape[3])
    full_y = groups_y * cylen
    full_z = groups_z * czlen
    each = -(-3 * cxlen // devices)
    table_x = cas_table(cxlen)
    table_y = cas_table(full_y)
    table_z = cas_table(full_z)
    coeffs = jnp.einsum("xi,cijk->cxjk", table_x, restricted, precision=HIGH)
    coeffs = coeffs.reshape(3 * cxlen, cylen, czlen)
    coeffs = jnp.pad(coeffs, ((0, each * devices - 3 * cxlen), (0, 0), (0, 0)))
    planes = lax.all_to_all(coeffs, both, 0, 0, tiled=True)
    planes = planes.reshape(groups_z, groups_y, each, cylen, czlen)
    planes = planes.transpose(2, 1, 3, 0, 4).reshape(each, full_y, full_z)
    planes = jnp.einsum("yj,pjk->pyk", table_y, planes, precision=HIGH)
    planes = jnp.einsum("zk,pyk->pyz", table_z, planes, precision=HIGH)
    line_x = jnp.tile(eigen_line(cxlen), -(-each * devices // cxlen))
    line_x = lax.dynamic_slice_in_dim(line_x, lax.axis_index(both) * each, each, 0)
    total = (
        line_x[:, None, None] + eigen_line(full_y)[None, :, None] + eigen_line(full_z)[None, None, :]
    )
    planes = planes / (GAMMA + COARSE_BETA * total * total)
    planes = jnp.einsum("zk,pyk->pyz", table_z, planes, precision=HIGH)
    planes = jnp.einsum("yj,pjk->pyk", table_y, planes, precision=HIGH)
    planes = planes.reshape(each, groups_y, cylen, groups_z, czlen).transpose(3, 1, 0, 2, 4)
    planes = planes.reshape(devices * each, cylen, czlen)
    coeffs = lax.all_to_all(planes, both, 0, 0, tiled=True)[: 3 * cxlen]
    coeffs = coeffs.reshape(3, cxlen, cylen, czlen)
    coeffs = jnp.einsum("xi,cijk->cxjk", table_x, coeffs, precision=HIGH)
    return coeffs / float(cxlen * full_y * full_z)


def lane_curve(left, right):
    spot = lax.broadcasted_iota(jnp.int32, left.shape, 2) % GROUP
    rims = jnp.where(spot < 2, left, right)
    rows = rims.shape[1]
    empty = jnp.zeros_like(rims[:, :1])
    up = jnp.concatenate([rims[:, 1:], empty], axis=1)
    down = jnp.concatenate([empty, rims[:, : rows - 1]], axis=1)
    bent = -2.0 * (
        6.0 * rims - jnp.roll(rims, GROUP, 2) - jnp.roll(rims, -GROUP, 2) - up - down
    )
    plain = jnp.where(spot < 2, jnp.roll(rims, -2, 2), jnp.roll(rims, 2, 2))
    curve = jnp.where(spot == 1, jnp.roll(bent, -1, 2), jnp.roll(bent, 1, 2))
    return BETA * (plain + jnp.where((spot == 1) | (spot == 2), curve, 0.0))


def per_device(velocity, increment, template, deformed):
    xlen, rows = template.shape[0], template.shape[1]

    packed, low, high = state_rims(template, deformed)
    packed, low, high, table = lax.optimization_barrier((packed, low, high, stencil_table()))
    left = shifted(packed, "gz", 1)
    right = shifted(packed, "gz", -1)
    lows = shifted(high, "gy", 1)
    highs = shifted(low, "gy", -1)

    inc_packed, inc_low, inc_high, low_curve, high_curve, filtered = stencil(increment, table)
    inc_packed, inc_low, inc_high, left, right, lows, highs = lax.optimization_barrier(
        (inc_packed, inc_low, inc_high, left, right, lows, highs)
    )
    inc_left = shifted(inc_packed, "gz", 1)
    inc_right = shifted(inc_packed, "gz", -1)
    inc_lows = shifted(inc_high, "gy", 1)
    inc_highs = shifted(inc_low, "gy", -1)

    s_packed, s_low, s_high, state, source, *pads = first_state(
        increment, template, deformed, lows, highs, left, right
    )
    s_left = shifted(s_packed, "gz", 1)
    s_right = shifted(s_packed, "gz", -1)
    s_below = shifted(s_high, "gy", 1)
    s_above = shifted(s_low, "gy", -1)

    inc_left, inc_right, inc_lows, inc_highs = lax.optimization_barrier(
        (inc_left, inc_right, inc_lows, inc_highs)
    )
    low_curve, high_curve = corners(low_curve, high_curve, inc_left, inc_right)
    s_left, s_right, s_below, s_above, low_curve, high_curve = lax.optimization_barrier(
        (s_left, s_right, s_below, s_above, low_curve, high_curve)
    )
    low_curves = shifted(high_curve, "gy", 1)
    high_curves = shifted(low_curve, "gy", -1)

    f_packed, f_low, f_high, adjoint = second_state(
        velocity, source, state, s_below, s_above, s_left, s_right
    )
    f_packed, low_curves, high_curves = lax.optimization_barrier(
        (f_packed, low_curves, high_curves)
    )
    f_left = shifted(f_packed, "gz", 1)
    f_right = shifted(f_packed, "gz", -1)
    f_below = shifted(f_high, "gy", 1)
    f_above = shifted(f_low, "gy", -1)

    filtered = edges_pass(
        filtered, inc_lows, inc_highs, low_curves, high_curves, lane_curve(inc_left, inc_right)
    )
    hessian, restricted = hessian_pass(
        filtered, velocity, adjoint, pads, f_below, f_above, f_left, f_right
    )
    coarse = coarse_spread(restricted.reshape(3, xlen // 4, rows // 4, LANES // 4))
    mixed = coarse.reshape(restricted.shape) - OMEGA * restricted
    return final_pass(hessian, mixed)


def solution(mesh):
    placed = (
        P(None, None, "gy", "gz"),
        P(None, None, "gy", "gz"),
        P(None, "gy", "gz"),
        P(None, "gy", "gz"),
    )
    return jax.shard_map(
        per_device, mesh=mesh, in_specs=placed, out_specs=P(None, None, "gy", "gz"), check_vma=False
    )
```

```python
import functools
import math

import jax
import jax.numpy as jnp
import numpy as np
from jax import lax
from jax.experimental import pallas as pl
from jax.experimental.pallas import tpu as pltpu
from jax.sharding import PartitionSpec as P

STEP = 0.5
BETA = 0.02
GAMMA = 0.05
COARSE_BETA = 0.025
OMEGA = 1.0 / (0.05 + 42.0 * 0.02)
HIGH = lax.Precision.HIGHEST

PART = 32
GROUP = 4
LANES = 128
TOP = 8
RUN = 8
BATCH = 32
LONG = 64
WIDE = 128
LARGE = 1 << 20


def shifted(value, axis, by):
    peers = lax.axis_size(axis)
    return lax.ppermute(value, axis, [(i, (i + by) % peers) for i in range(peers)])


def cas_table(count):
    index = np.arange(count)
    angle = (index[:, None] * index[None, :] % count) * (2.0 * math.pi / count)
    return jnp.asarray(np.cos(angle) + np.sin(angle), jnp.float32)


def eigen_line(count):
    return jnp.asarray(2.0 - 2.0 * np.cos(np.arange(count) * (2.0 * math.pi / count)), jnp.float32)


def lane_of(rows):
    return lax.broadcasted_iota(jnp.int32, (rows, LANES), 1)


def turn(value, by):
    return pltpu.roll(value, by % LANES if isinstance(by, int) else by, 1)


def turned_to(value, place):
    return pltpu.roll(value, lax.rem(place, LANES), 1)


def turned_from(value, place):
    return pltpu.roll(value, lax.rem(LANES - lax.rem(place, LANES), LANES), 1)


def z_sides(value, rim, lane):
    before = jnp.where(lane == 0, rim, turn(value, 1))
    after = jnp.where(lane == LANES - 1, rim, turn(value, -1))
    return before, after


def planes_loop(count, body, carry=0, step=RUN):
    def several(k, carry):
        for j in range(step):
            carry = body(k * step + j, carry)
        return carry

    return lax.fori_loop(0, count // step, several, carry)


def y_sides(value, low, high):
    rows = value.shape[0]
    row = lax.broadcasted_iota(jnp.int32, value.shape, 0)
    before = jnp.where(row == 0, low, pltpu.roll(value, 1, 0))
    after = jnp.where(row == rows - 1, high, pltpu.roll(value, rows - 1, 0))
    return before, after


def halves(value):
    large = value.astype(jnp.bfloat16)
    small = (value - large.astype(jnp.float32)).astype(jnp.bfloat16)
    return jnp.concatenate([large, small], axis=1)


def doubled(table):
    return jnp.asarray(np.concatenate([table, table], axis=0), jnp.bfloat16)


def product(left, right):
    return jnp.dot(left, right, preferred_element_type=jnp.float32)


def call(body, grid, streamed, kept, out_streamed, out_kept, scratch, flops, moved, grant=12, reused=None):
    counts = [len(streamed), len(kept), len(out_streamed), len(out_kept)]

    def kernel(*refs):
        groups = []
        for count in counts:
            groups.append(refs[:count])
            refs = refs[count:]

        def step(*blocks):
            body(*blocks[: counts[0]], *groups[1], *blocks[counts[0] :], *groups[3], *refs)

        pltpu.emit_pipeline(
            step,
            grid=grid,
            in_specs=[spec for _, spec in streamed],
            out_specs=[spec for _, spec in out_streamed],
        )(*groups[0], *groups[2])

    def placed(array):
        return pltpu.with_memory_space_constraint(array, pltpu.HBM) if array.size >= LARGE else array

    far = pl.BlockSpec(memory_space=pl.ANY)
    near = pl.BlockSpec(memory_space=pltpu.VMEM)
    return pl.pallas_call(
        kernel,
        in_specs=[far] * counts[0] + [near] * counts[1],
        out_specs=[far] * counts[2] + [near] * counts[3],
        out_shape=[jax.ShapeDtypeStruct(shape, jnp.float32) for shape, _ in out_streamed]
        + [pltpu.VMEM(shape, jnp.float32) for shape in out_kept],
        scratch_shapes=scratch,
        input_output_aliases={} if reused is None else {counts[0] + reused[0]: counts[2] + reused[1]},
        cost_estimate=pl.CostEstimate(flops=flops, bytes_accessed=moved, transcendentals=0),
        compiler_params=pltpu.CompilerParams(vmem_limit_bytes=grant * 1024 * 1024),
    )(
        *[placed(array) for array, _ in streamed],
        *[pltpu.with_memory_space_constraint(array, pltpu.VMEM) for array in kept],
    )


def state_rims_body(first, second, packed, low, high):
    rows = first.shape[1]
    lane = lane_of(rows)
    owner = lane // GROUP
    spot = lane % GROUP

    def plane(base, part, edge):
        i = base + part
        a = first[i].astype(jnp.float32)
        b = second[i].astype(jnp.float32)
        low[0, pl.ds(i, 1), :] = a[:1]
        low[1, pl.ds(i, 1), :] = b[:1]
        high[0, pl.ds(i, 1), :] = a[rows - 1 :]
        high[1, pl.ds(i, 1), :] = b[rows - 1 :]
        both = jnp.where(spot < 2, turned_to(a, GROUP * part + 1), turned_to(b, GROUP * part + 3))
        return jnp.where(owner == part, both, edge)

    for b in range(LONG // PART):
        packed[:, b * LANES : (b + 1) * LANES] = planes_loop(
            PART, functools.partial(plane, b * PART), jnp.zeros((rows, LANES), jnp.float32), PART
        )


def state_rims(first, second):
    xlen, rows = first.shape[0], first.shape[1]
    block = pl.BlockSpec((LONG, rows, LANES), lambda i: (i, 0, 0))
    slab = pl.BlockSpec((2, LONG, LANES), lambda i: (0, i, 0))
    return call(
        state_rims_body,
        (xlen // LONG,),
        [(first, block), (second, block)],
        [],
        [
            ((rows, GROUP * xlen), pl.BlockSpec((rows, LONG // PART * LANES), lambda i: (0, i))),
            ((2, xlen, LANES), slab),
            ((2, xlen, LANES), slab),
        ],
        [],
        [],
        8 * first.size,
        4 * first.size,
    )


def stencil_table():
    cell = np.arange(LANES)
    gap = np.abs(cell[:, None] - cell[None, :])
    outer = np.where(gap == 0, 38.0, np.where(gap == 1, -12.0, np.where(gap == 2, 1.0, 0.0)))
    inner = np.where(gap == 0, -12.0, np.where(gap == 1, 2.0, 0.0))
    table = np.concatenate([outer, inner], axis=1)
    return doubled(table)


def stencil_body(
    before, cells, after, table, packed, low, high, low_curve, high_curve, out, padded, inner
):
    rows = cells.shape[2]
    comp = pl.program_id(0)
    base = pl.program_id(1) * LONG
    owner = lane_of(rows) // GROUP
    here = pl.ds(TOP, rows)

    @pl.when((comp == 0) & (base == 0))
    def _():
        padded[...] = jnp.zeros_like(padded)

    for j in range(2):
        padded[j, here] = before[0, j]
        padded[LONG + 2 + j, here] = after[0, j]

    def fill(i, carry):
        padded[i + 2, here] = cells[0, i]
        return carry

    planes_loop(LONG, fill)

    def middle(j, count):
        flat = padded[pl.ds(j, count), here].reshape(count * rows, LANES)
        both = product(halves(flat), table[...])
        found = []
        for k in range(count):
            value = padded[j + k, here]
            part = both[k * rows : (k + 1) * rows]
            along = padded[j + k - 1, here] + padded[j + k + 1, here]
            core = (
                part[:, LANES:]
                + along
                + (padded[j + k, pl.ds(TOP - 1, rows)] + padded[j + k, pl.ds(TOP + 1, rows)])
            )
            inner[j + k - 1, here] = core
            inner[j + k - 1, TOP - 1 : TOP] = value[:1]
            inner[j + k - 1, TOP + rows : TOP + rows + 1] = value[rows - 1 :]
            found.append((value, part[:, :LANES], core, along))
        return found

    middle(1, 1)
    middle(LONG + 2, 1)

    for b in range(LONG // PART):

        def several(k, edge):
            first = b * PART + k * BATCH
            for j, (value, outer, core, along) in enumerate(middle(first + 2, BATCH)):
                i = first + j
                out[comp, base + i] = GAMMA * value + BETA * outer
                low[0, pl.ds(i, 1), :] = value[:1]
                high[0, pl.ds(i, 1), :] = value[rows - 1 :]
                low_curve[0, pl.ds(i, 1), :] = core[:1] + along[:1]
                high_curve[0, pl.ds(i, 1), :] = core[rows - 1 :] + along[rows - 1 :]
                part = k * BATCH + j
                edge = jnp.where(owner == part, turned_to(value, GROUP * part + 2), edge)
            return edge

        packed[0, :, b * LANES : (b + 1) * LANES] = lax.fori_loop(
            0, PART // BATCH, several, jnp.zeros((rows, LANES), jnp.float32)
        )

    def finish(i, carry):
        around = (inner[i, here] + inner[i + 2, here]) + (
            inner[i + 1, pl.ds(TOP - 1, rows)] + inner[i + 1, pl.ds(TOP + 1, rows)]
        )
        out[comp, base + i] = out[comp, base + i] + BETA * around
        return carry

    planes_loop(LONG, finish)


def stencil(increment, table):
    parts, xlen, rows = increment.shape[:3]
    half = LONG // 2
    pairs = xlen // 2
    slab = pl.BlockSpec((1, LONG, LANES), lambda c, i: (c, i, 0))
    return call(
        stencil_body,
        (parts, xlen // LONG),
        [
            (
                increment,
                pl.BlockSpec(
                    (1, 2, rows, LANES),
                    lambda c, i: (c, lax.rem(half * i + pairs - 1, pairs), 0, 0),
                ),
            ),
            (increment, pl.BlockSpec((1, LONG, rows, LANES), lambda c, i: (c, i, 0, 0))),
            (
                increment,
                pl.BlockSpec(
                    (1, 2, rows, LANES), lambda c, i: (c, lax.rem(half * i + half, pairs), 0, 0)
                ),
            ),
        ],
        [table],
        [
            (
                (parts, rows, GROUP * xlen),
                pl.BlockSpec((1, rows, LONG // PART * LANES), lambda c, i: (c, 0, i)),
            ),
        ]
        + [((parts, xlen, LANES), slab)] * 4,
        [increment.shape],
        [
            pltpu.VMEM((LONG + 4, rows + 2 * TOP, LANES), jnp.float32),
            pltpu.VMEM((LONG + 2, rows + 2 * TOP, LANES), jnp.float32),
        ],
        24 * increment.size,
        4 * increment.size,
        12,
    )


def corner_table():
    table = np.zeros((LANES, LANES))
    table[1::GROUP, 0] = 2.0
    table[2::GROUP, LANES - 1] = 2.0
    return table


def corner_body(low, high, left, right, table, out_low, out_high):
    parts, xlen = low.shape[:2]
    rows = left.shape[1]
    row = lax.broadcasted_iota(jnp.int32, (PART, LANES), 0)
    lane = lax.broadcasted_iota(jnp.int32, (PART, LANES), 1)
    mine = lane // GROUP == row
    for c in range(parts):
        for b in range(xlen // PART):
            planes = slice(b * PART, (b + 1) * PART)
            lanes = slice(b * LANES, (b + 1) * LANES)
            for curve, out, at in ((low, out_low, 0), (high, out_high, rows - 1)):
                rim = jnp.where(
                    lane % GROUP == 1, left[c, at : at + 1, lanes], right[c, at : at + 1, lanes]
                )
                rim = halves(jnp.where(mine, rim, 0.0))
                out[c, planes] = BETA * (curve[c, planes] + product(rim, table[...]))


def corners(low, high, left, right):
    near = pl.BlockSpec(memory_space=pltpu.VMEM)
    return pl.pallas_call(
        corner_body,
        in_specs=[near] * 5,
        out_specs=[near] * 2,
        out_shape=[jax.ShapeDtypeStruct(low.shape, jnp.float32)] * 2,
        cost_estimate=pl.CostEstimate(
            flops=8 * low.size, bytes_accessed=16 * low.size, transcendentals=0
        ),
        compiler_params=pltpu.CompilerParams(vmem_limit_bytes=12 * 1024 * 1024),
    )(low, high, left, right, doubled(corner_table()))


def edges_body(
    low, high, low_curve, high_curve, lanes, filtered, out,
):
    rows = filtered.shape[2]
    base = pl.program_id(0) * PART
    lane = lane_of(rows)
    row = lax.broadcasted_iota(jnp.int32, (8, LANES), 0)
    outer = (lane < 2) | (lane >= LANES - 2)
    for d in range(3):

        def plane(i, carry):
            at = pl.ds(i, 1)
            cyclic = turned_from(lanes[d], GROUP * i + 2)
            value = filtered[d, base + i] + jnp.where(outer, cyclic, 0.0)
            first = jnp.where(row == 1, BETA * low[d, at], 0.0)
            first = jnp.where(row == 0, low_curve[d, at], first)
            last = jnp.where(row == 6, BETA * high[d, at], 0.0)
            last = jnp.where(row == 7, high_curve[d, at], last)
            if rows == 8:
                out[d, base + i] = value + first + last
            else:
                out[d, base + i, :8] = value[:8] + first
                out[d, base + i, 8 : rows - 8] = value[8 : rows - 8]
                out[d, base + i, rows - 8 :] = value[rows - 8 :] + last
            return carry

        planes_loop(PART, plane, 0, 32)


def edges_pass(filtered, low, high, low_curve, high_curve, lanes):
    parts, xlen, rows = filtered.shape[:3]
    slab = pl.BlockSpec((parts, PART, LANES), lambda i: (0, i, 0))
    return call(
        edges_body,
        (xlen // PART,),
        [(low, slab), (high, slab), (low_curve, slab), (high_curve, slab)]
        + [(lanes, pl.BlockSpec((parts, rows, LANES), lambda i: (0, 0, i)))],
        [filtered],
        [],
        [filtered.shape],
        [],
        4 * filtered.size,
        filtered.size,
        4,
        (0, 0),
    )[0]


def gradient_table():
    cell = np.arange(LANES)
    gap = cell[None, :] - cell[:, None]
    slope = (gap == -1).astype(np.float64) - (gap == 1)
    none = np.zeros_like(slope)
    rims = np.zeros((LANES, 2 * LANES))
    rims[0::GROUP, 0] = -1.0
    rims[1::GROUP, LANES - 1] = 1.0
    rims[2::GROUP, LANES] = -1.0
    rims[3::GROUP, 2 * LANES - 1] = 1.0
    return jnp.asarray(np.block([[slope, none], [none, slope], [rims]]), jnp.bfloat16)


def load_states(m0, m0b, m0a, m1, m1b, m1a, lows, highs, rims, table, pad0, pad1, slopes):
    rows = m0.shape[1]
    base = pl.program_id(0) * PART
    here = pl.ds(TOP, rows)
    owner = lane_of(rows) // GROUP
    for which, (ref, before, after, pad) in enumerate(((m0, m0b, m0a, pad0), (m1, m1b, m1a, pad1))):

        @pl.when(base == 0)
        def _():
            pad[0, here] = before[0].astype(jnp.float32)

        pad[base + PART + 1, here] = after[0].astype(jnp.float32)

        def fill(i, carry):
            pad[base + i + 1, here] = ref[i].astype(jnp.float32)
            pad[base + i + 1, pl.ds(TOP - 1, 1)] = lows[which, pl.ds(i, 1), :]
            pad[base + i + 1, pl.ds(TOP + rows, 1)] = highs[which, pl.ds(i, 1), :]
            return carry

        planes_loop(PART, fill)

    def several(k, carry):
        first = k * BATCH
        flat = [
            pad[pl.ds(base + first + 1, BATCH), here].reshape(BATCH * rows, LANES).astype(jnp.bfloat16)
            for pad in (pad0, pad1)
        ]
        edge = jnp.concatenate([jnp.where(owner == first + j, rims, 0.0) for j in range(BATCH)], axis=0)
        both = product(jnp.concatenate(flat + [edge.astype(jnp.bfloat16)], axis=1), table[...])
        slopes[pl.ds(base + first, BATCH)] = both.reshape(BATCH, rows, 2 * LANES)
        return carry

    lax.fori_loop(0, PART // BATCH, several, 0)


def gradients(pad, slope, i, rows):
    here = pl.ds(TOP, rows)
    return (
        pad[i + 2, here] - pad[i, here],
        pad[i + 1, pl.ds(TOP + 1, rows)] - pad[i + 1, pl.ds(TOP - 1, rows)],
        slope,
    )


def crossed_rims(left, right, rows):
    rims = merged_rims(left, right, rows)
    return jnp.where(lane_of(rows) % 2 == 0, turn(rims, -1), turn(rims, 1))


def merged_rims(left, right, rows):
    spot = lane_of(rows) % GROUP
    return jnp.where(spot % 2 == 0, left[...], right[...])


def first_state_body(
    increment, m0, m0b, m0a, m1, m1b, m1a, lows, highs, left, right, table,
    packed, low, high, state, source, pad0, pad1, slopes,
):
    rows = m0.shape[1]
    base = pl.program_id(0) * PART
    owner = lane_of(rows) // GROUP
    rims = merged_rims(left, right, rows)
    load_states(m0, m0b, m0a, m1, m1b, m1a, lows, highs, rims, table, pad0, pad1, slopes)

    def plane(i, edge):
        g0 = gradients(pad0, slopes[base + i, :, :LANES], base + i, rows)
        g1 = gradients(pad1, slopes[base + i, :, LANES:], base + i, rows)
        u = [increment[d, i] for d in range(3)]
        one = (-0.5 * STEP) * (u[0] * g0[0] + u[1] * g0[1] + u[2] * g0[2])
        state[base + i] = one
        source[base + i] = (0.5 * STEP) * (u[0] * g1[0] + u[1] * g1[1] + u[2] * g1[2])
        low[pl.ds(i, 1), :] = one[:1]
        high[pl.ds(i, 1), :] = one[rows - 1 :]
        return jnp.where(owner == i, turned_to(one, GROUP * i + 1), edge)

    packed[...] = planes_loop(PART, plane, jnp.zeros((rows, LANES), jnp.float32), 32)


def around(array):
    xlen, rows = array.shape[:2]
    return [
        (array, pl.BlockSpec((PART, rows, LANES), lambda i: (i, 0, 0))),
        (array, pl.BlockSpec((1, rows, LANES), lambda i: (lax.rem(PART * i + xlen - 1, xlen), 0, 0))),
        (array, pl.BlockSpec((1, rows, LANES), lambda i: (lax.rem(PART * i + PART, xlen), 0, 0))),
    ]


def first_state(increment, first, second, lows, highs, left, right):
    xlen, rows = first.shape[0], first.shape[1]
    triple = pl.BlockSpec((3, PART, rows, LANES), lambda i: (0, i, 0, 0))
    slab = pl.BlockSpec((PART, LANES), lambda i: (i, 0))
    double = pl.BlockSpec((2, PART, LANES), lambda i: (0, i, 0))
    rim = pl.BlockSpec((rows, LANES), lambda i: (0, i))
    return call(
        first_state_body,
        (xlen // PART,),
        [(increment, triple)]
        + around(first)
        + around(second)
        + [(lows, double), (highs, double), (left, rim), (right, rim)],
        [gradient_table()],
        [((rows, GROUP * xlen), rim), ((xlen, LANES), slab), ((xlen, LANES), slab)],
        [first.shape, first.shape]
        + [(xlen + 2, rows + 2 * TOP, LANES)] * 2
        + [(xlen, rows, 2 * LANES)],
        [],
        24 * first.size,
        16 * first.size,
        6,
    )


def second_state_body(
    velocity, low, high, left, right, state, source, packed, out_low, out_high, adjoint, across
):
    xlen, rows = state.shape[0], state.shape[1]
    base = pl.program_id(0) * PART
    lane = lane_of(rows)
    owner = lane // GROUP
    rims = crossed_rims(left, right, rows)

    def lanes_part(i, carry):
        value = state[base + i]
        speed = velocity[2, i]
        before, after = z_sides(value, turned_from(rims, GROUP * i + 1), lane)
        across[i] = (STEP * speed) * jnp.where(speed > 0.0, value - before, after - value)
        return carry

    planes_loop(PART, lanes_part, 0, 32)

    def plane(i, edge):
        value = state[base + i]
        total = (source[base + i] - value) + across[i]
        sides = [
            (
                state[lax.rem(base + i + xlen - 1, xlen)],
                state[lax.rem(base + i + 1, xlen)],
            ),
            y_sides(value, low[pl.ds(i, 1), :], high[pl.ds(i, 1), :]),
        ]
        for d in range(2):
            speed = velocity[d, i]
            slope = jnp.where(speed > 0.0, value - sides[d][0], sides[d][1] - value)
            total = total + (STEP * speed) * slope
        adjoint[base + i] = total
        along = velocity[1, i]
        out_low[pl.ds(i, 1), :] = jnp.maximum(along[:1], 0.0) * total[:1]
        out_high[pl.ds(i, 1), :] = jnp.minimum(along[rows - 1 :], 0.0) * total[rows - 1 :]
        along = velocity[2, i]
        flow = total * jnp.where(
            lane == LANES - 1, jnp.minimum(along, 0.0), jnp.maximum(along, 0.0)
        )
        return jnp.where(owner == i, turned_to(flow, GROUP * i + 1), edge)

    packed[...] = planes_loop(PART, plane, jnp.zeros((rows, LANES), jnp.float32), 32)


def second_state(velocity, source, state, low, high, left, right):
    xlen, rows = state.shape[0], state.shape[1]
    triple = pl.BlockSpec((3, PART, rows, LANES), lambda i: (0, i, 0, 0))
    slab = pl.BlockSpec((PART, LANES), lambda i: (i, 0))
    rim = pl.BlockSpec((rows, LANES), lambda i: (0, i))
    return call(
        second_state_body,
        (xlen // PART,),
        [(velocity, triple), (low, slab), (high, slab), (left, rim), (right, rim)],
        [state, source],
        [((rows, GROUP * xlen), rim), ((xlen, LANES), slab), ((xlen, LANES), slab)],
        [state.shape],
        [pltpu.VMEM((PART, rows, LANES), jnp.float32)],
        30 * state.size,
        12 * state.size,
        6,
        (1, 0),
    )


def fold_table(count):
    return np.repeat(np.eye(count), 4, axis=1)


def hessian_body(
    velocity, speed_b, speed_a, flow_low, flow_high, flow_left, flow_right,
    filtered, adjoint, pad0, pad1, slopes, fold_z, out, restricted, flows, sums, few,
):
    xlen, rows = adjoint.shape[0], adjoint.shape[1]
    base = pl.program_id(0) * PART
    lane = lane_of(rows)
    row = lax.broadcasted_iota(jnp.int32, (rows, LANES), 0)
    ends = crossed_rims(flow_left, flow_right, rows)

    def across(i, carry):
        value = adjoint[base + i]
        speed = velocity[2, i]
        rim = turned_from(ends, GROUP * i + 1)
        later = turn(jnp.maximum(speed, 0.0) * value, -1)
        prev = turn(jnp.minimum(speed, 0.0) * value, 1)
        flows[i] = jnp.where(lane == LANES - 1, rim, later) - jnp.where(lane == 0, rim, prev)
        return carry

    planes_loop(PART, across, 0, 32)

    def plane(i, carry):
        g0 = gradients(pad0, slopes[base + i, :, :LANES], base + i, rows)
        g1 = gradients(pad1, slopes[base + i, :, LANES:], base + i, rows)
        value = adjoint[base + i]
        sx, sy, sz = (velocity[d, i] for d in range(3))
        before, after = jnp.maximum(i - 1, 0), jnp.minimum(i + 1, PART - 1)
        speed_before = jnp.where(i == 0, speed_b[0, 0], velocity[0, before])
        speed_after = jnp.where(i == PART - 1, speed_a[0, 0], velocity[0, after])
        prev = jnp.minimum(speed_before, 0.0) * adjoint[lax.rem(base + i + xlen - 1, xlen)]
        later = jnp.maximum(speed_after, 0.0) * adjoint[lax.rem(base + i + 1, xlen)]
        inflow = pltpu.roll(jnp.minimum(sy, 0.0) * value, 1, 0)
        outflow = pltpu.roll(jnp.maximum(sy, 0.0) * value, rows - 1, 0)
        change = (
            (later - prev)
            + flows[i]
            + jnp.where(row == rows - 1, flow_high[pl.ds(i, 1), :], outflow)
            - jnp.where(row == 0, flow_low[pl.ds(i, 1), :], inflow)
            - (jnp.abs(sx) + jnp.abs(sy) + jnp.abs(sz)) * value
        )
        half_two = (0.5 * STEP) * value
        half_one = half_two + (0.5 * STEP * STEP) * change
        for d in range(3):
            out[d, i] = filtered[d, base + i] + half_one * g0[d] + half_two * g1[d]
        return carry

    planes_loop(PART, plane, 0, 16)

    count = PART // 4 * (rows // 4)
    for d in range(3):

        def fold(k, carry):
            total = (out[d, 4 * k] + out[d, 4 * k + 1]) + (out[d, 4 * k + 2] + out[d, 4 * k + 3])
            total = total + pltpu.roll(total, rows - 1, 0)
            sums[pl.ds(k * rows, rows)] = total + pltpu.roll(total, rows - 2, 0)
            return carry

        planes_loop(PART // 4, fold)
        few[pl.ds(d * count, count)] = sums[pl.ds(0, count, stride=4)]
    found = product(halves(few[...]), fold_z[...]) * (1.0 / 64.0)
    restricted[...] = found.reshape(3, count, LANES // 4)


def hessian_pass(
    filtered, velocity, adjoint, pads, flow_low, flow_high, flow_left, flow_right,
):
    xlen, rows = adjoint.shape[0], adjoint.shape[1]
    triple = pl.BlockSpec((3, PART, rows, LANES), lambda i: (0, i, 0, 0))
    slab = pl.BlockSpec((PART, LANES), lambda i: (i, 0))
    rim = pl.BlockSpec((rows, LANES), lambda i: (0, i))
    speed_b = pl.BlockSpec(
        (1, 1, rows, LANES), lambda i: (0, lax.rem(PART * i + xlen - 1, xlen), 0, 0)
    )
    speed_a = pl.BlockSpec((1, 1, rows, LANES), lambda i: (0, lax.rem(PART * i + PART, xlen), 0, 0))
    coarse_rows = PART // 4 * (rows // 4)
    return call(
        hessian_body,
        (xlen // PART,),
        [(velocity, triple), (velocity, speed_b), (velocity, speed_a)]
        + [(flow_low, slab), (flow_high, slab), (flow_left, rim), (flow_right, rim)],
        [filtered, adjoint, *pads, doubled(fold_table(LANES // 4).T)],
        [
            (filtered.shape, triple),
            (
                (3, xlen // 4 * (rows // 4), LANES // 4),
                pl.BlockSpec((3, coarse_rows, LANES // 4), lambda i: (0, i, 0)),
            ),
        ],
        [],
        [
            pltpu.VMEM((PART, rows, LANES), jnp.float32),
            pltpu.VMEM((PART // 4 * rows, LANES), jnp.float32),
            pltpu.VMEM((3 * coarse_rows, LANES), jnp.float32),
        ],
        70 * adjoint.size,
        24 * adjoint.size,
        9,
    )


def final_body(coarse, hessian, spread_z, out, wide):
    rows = hessian.shape[2]
    few = rows // 4
    wide[...] = product(halves(coarse[0]), spread_z[...])
    half = lax.broadcasted_iota(jnp.int32, (8, LANES), 0) < 4

    def fold(k, carry):
        add = [
            jnp.where(
                half, wide[pl.ds(k * few + 2 * r, 1), :], wide[pl.ds(k * few + 2 * r + 1, 1), :]
            )
            for r in range(rows // 8)
        ]
        add = jnp.concatenate(add, axis=0)
        for j in range(4):
            out[0, 4 * k + j] = OMEGA * hessian[0, 4 * k + j] + add
        return carry

    planes_loop(WIDE // 4, fold, 0, 2)


def final_pass(hessian, coarse):
    parts, xlen, rows = hessian.shape[:3]
    block = pl.BlockSpec((1, WIDE, rows, LANES), lambda c, i: (c, i, 0, 0))
    coarse_rows = WIDE // 4 * (rows // 4)
    return call(
        final_body,
        (parts, xlen // WIDE),
        [
            (coarse, pl.BlockSpec((1, coarse_rows, LANES // 4), lambda c, i: (c, i, 0))),
            (hessian, block),
        ],
        [doubled(fold_table(LANES // 4))],
        [(hessian.shape, block)],
        [],
        [pltpu.VMEM((coarse_rows, LANES), jnp.float32)],
        2 * hessian.size,
        8 * hessian.size,
        20,
    )[0]


def coarse_spread(restricted):
    both = ("gz", "gy")
    groups_z = lax.axis_size("gz")
    groups_y = lax.axis_size("gy")
    devices = groups_z * groups_y
    cxlen, cylen, czlen = (restricted.shape[1], restricted.shape[2], restricted.shape[3])
    full_y = groups_y * cylen
    full_z = groups_z * czlen
    each = -(-3 * cxlen // devices)
    table_x = cas_table(cxlen)
    table_y = cas_table(full_y)
    table_z = cas_table(full_z)
    coeffs = jnp.einsum("xi,cijk->cxjk", table_x, restricted, precision=HIGH)
    coeffs = coeffs.reshape(3 * cxlen, cylen, czlen)
    coeffs = jnp.pad(coeffs, ((0, each * devices - 3 * cxlen), (0, 0), (0, 0)))
    planes = lax.all_to_all(coeffs, both, 0, 0, tiled=True)
    planes = planes.reshape(groups_z, groups_y, each, cylen, czlen)
    planes = planes.transpose(2, 1, 3, 0, 4).reshape(each, full_y, full_z)
    planes = jnp.einsum("yj,pjk->pyk", table_y, planes, precision=HIGH)
    planes = jnp.einsum("zk,pyk->pyz", table_z, planes, precision=HIGH)
    line_x = jnp.tile(eigen_line(cxlen), -(-each * devices // cxlen))
    line_x = lax.dynamic_slice_in_dim(line_x, lax.axis_index(both) * each, each, 0)
    total = (
        line_x[:, None, None] + eigen_line(full_y)[None, :, None] + eigen_line(full_z)[None, None, :]
    )
    planes = planes / (GAMMA + COARSE_BETA * total * total)
    planes = jnp.einsum("zk,pyk->pyz", table_z, planes, precision=HIGH)
    planes = jnp.einsum("yj,pjk->pyk", table_y, planes, precision=HIGH)
    planes = planes.reshape(each, groups_y, cylen, groups_z, czlen).transpose(3, 1, 0, 2, 4)
    planes = planes.reshape(devices * each, cylen, czlen)
    coeffs = lax.all_to_all(planes, both, 0, 0, tiled=True)[: 3 * cxlen]
    coeffs = coeffs.reshape(3, cxlen, cylen, czlen)
    coeffs = jnp.einsum("xi,cijk->cxjk", table_x, coeffs, precision=HIGH)
    return coeffs / float(cxlen * full_y * full_z)


def lane_curve(left, right):
    spot = lax.broadcasted_iota(jnp.int32, left.shape, 2) % GROUP
    rims = jnp.where(spot < 2, left, right)
    rows = rims.shape[1]
    empty = jnp.zeros_like(rims[:, :1])
    up = jnp.concatenate([rims[:, 1:], empty], axis=1)
    down = jnp.concatenate([empty, rims[:, : rows - 1]], axis=1)
    bent = -2.0 * (
        6.0 * rims - jnp.roll(rims, GROUP, 2) - jnp.roll(rims, -GROUP, 2) - up - down
    )
    plain = jnp.where(spot < 2, jnp.roll(rims, -2, 2), jnp.roll(rims, 2, 2))
    curve = jnp.where(spot == 1, jnp.roll(bent, -1, 2), jnp.roll(bent, 1, 2))
    return BETA * (plain + jnp.where((spot == 1) | (spot == 2), curve, 0.0))


def per_device(velocity, increment, template, deformed):
    xlen, rows = template.shape[0], template.shape[1]

    packed, low, high = state_rims(template, deformed)
    packed, low, high, table = lax.optimization_barrier((packed, low, high, stencil_table()))
    left = shifted(packed, "gz", 1)
    right = shifted(packed, "gz", -1)
    lows = shifted(high, "gy", 1)
    highs = shifted(low, "gy", -1)

    inc_packed, inc_low, inc_high, low_curve, high_curve, filtered = stencil(increment, table)
    inc_packed, inc_low, inc_high, left, right, lows, highs = lax.optimization_barrier(
        (inc_packed, inc_low, inc_high, left, right, lows, highs)
    )
    inc_left = shifted(inc_packed, "gz", 1)
    inc_right = shifted(inc_packed, "gz", -1)
    inc_lows = shifted(inc_high, "gy", 1)
    inc_highs = shifted(inc_low, "gy", -1)

    s_packed, s_low, s_high, state, source, *pads = first_state(
        increment, template, deformed, lows, highs, left, right
    )
    s_left = shifted(s_packed, "gz", 1)
    s_right = shifted(s_packed, "gz", -1)
    s_below = shifted(s_high, "gy", 1)
    s_above = shifted(s_low, "gy", -1)

    inc_left, inc_right, inc_lows, inc_highs = lax.optimization_barrier(
        (inc_left, inc_right, inc_lows, inc_highs)
    )
    low_curve, high_curve = corners(low_curve, high_curve, inc_left, inc_right)
    s_left, s_right, s_below, s_above, low_curve, high_curve = lax.optimization_barrier(
        (s_left, s_right, s_below, s_above, low_curve, high_curve)
    )
    low_curves = shifted(high_curve, "gy", 1)
    high_curves = shifted(low_curve, "gy", -1)

    f_packed, f_low, f_high, adjoint = second_state(
        velocity, source, state, s_below, s_above, s_left, s_right
    )
    f_packed, low_curves, high_curves = lax.optimization_barrier(
        (f_packed, low_curves, high_curves)
    )
    f_left = shifted(f_packed, "gz", 1)
    f_right = shifted(f_packed, "gz", -1)
    f_below = shifted(f_high, "gy", 1)
    f_above = shifted(f_low, "gy", -1)

    filtered = edges_pass(
        filtered, inc_lows, inc_highs, low_curves, high_curves, lane_curve(inc_left, inc_right)
    )
    hessian, restricted = hessian_pass(
        filtered, velocity, adjoint, pads, f_below, f_above, f_left, f_right
    )
    coarse = coarse_spread(restricted.reshape(3, xlen // 4, rows // 4, LANES // 4))
    mixed = coarse.reshape(restricted.shape) - OMEGA * restricted
    return final_pass(hessian, mixed)


def solution(mesh):
    placed = (
        P(None, None, "gy", "gz"),
        P(None, None, "gy", "gz"),
        P(None, "gy", "gz"),
        P(None, "gy", "gz"),
    )
    return jax.shard_map(
        per_device, mesh=mesh, in_specs=placed, out_specs=P(None, None, "gy", "gz"), check_vma=False
    )
```

```python
import functools
import math

import jax
import jax.numpy as jnp
import numpy as np
from jax import lax
from jax.experimental import pallas as pl
from jax.experimental.pallas import tpu as pltpu
from jax.sharding import PartitionSpec as P

STEP = 0.5
BETA = 0.02
GAMMA = 0.05
COARSE_BETA = 0.025
OMEGA = 1.0 / (0.05 + 42.0 * 0.02)
HIGH = lax.Precision.HIGHEST

PART = 32
GROUP = 4
LANES = 128
TOP = 8
RUN = 8
BATCH = 32
LONG = 64
WIDE = 128
LARGE = 1 << 20


def shifted(value, axis, by):
    peers = lax.axis_size(axis)
    return lax.ppermute(value, axis, [(i, (i + by) % peers) for i in range(peers)])


def cas_table(count):
    index = np.arange(count)
    angle = (index[:, None] * index[None, :] % count) * (2.0 * math.pi / count)
    return jnp.asarray(np.cos(angle) + np.sin(angle), jnp.float32)


def eigen_line(count):
    return jnp.asarray(2.0 - 2.0 * np.cos(np.arange(count) * (2.0 * math.pi / count)), jnp.float32)


def lane_of(rows):
    return lax.broadcasted_iota(jnp.int32, (rows, LANES), 1)


def turn(value, by):
    return pltpu.roll(value, by % LANES if isinstance(by, int) else by, 1)


def turned_to(value, place):
    return pltpu.roll(value, lax.rem(place, LANES), 1)


def turned_from(value, place):
    return pltpu.roll(value, lax.rem(LANES - lax.rem(place, LANES), LANES), 1)


def z_sides(value, rim, lane):
    before = jnp.where(lane == 0, rim, turn(value, 1))
    after = jnp.where(lane == LANES - 1, rim, turn(value, -1))
    return before, after


def planes_loop(count, body, carry=0, step=RUN):
    def several(k, carry):
        for j in range(step):
            carry = body(k * step + j, carry)
        return carry

    return lax.fori_loop(0, count // step, several, carry)


def y_sides(value, low, high):
    rows = value.shape[0]
    row = lax.broadcasted_iota(jnp.int32, value.shape, 0)
    before = jnp.where(row == 0, low, pltpu.roll(value, 1, 0))
    after = jnp.where(row == rows - 1, high, pltpu.roll(value, rows - 1, 0))
    return before, after


def halves(value):
    large = value.astype(jnp.bfloat16)
    small = (value - large.astype(jnp.float32)).astype(jnp.bfloat16)
    return jnp.concatenate([large, small], axis=1)


def doubled(table):
    return jnp.asarray(np.concatenate([table, table], axis=0), jnp.bfloat16)


def product(left, right):
    return jnp.dot(left, right, preferred_element_type=jnp.float32)


def call(body, grid, streamed, kept, out_streamed, out_kept, scratch, flops, moved, grant=12, reused=None):
    counts = [len(streamed), len(kept), len(out_streamed), len(out_kept)]

    def kernel(*refs):
        groups = []
        for count in counts:
            groups.append(refs[:count])
            refs = refs[count:]

        def step(*blocks):
            body(*blocks[: counts[0]], *groups[1], *blocks[counts[0] :], *groups[3], *refs)

        pltpu.emit_pipeline(
            step,
            grid=grid,
            in_specs=[spec for _, spec in streamed],
            out_specs=[spec for _, spec in out_streamed],
        )(*groups[0], *groups[2])

    def placed(array):
        return pltpu.with_memory_space_constraint(array, pltpu.HBM) if array.size >= LARGE else array

    far = pl.BlockSpec(memory_space=pl.ANY)
    near = pl.BlockSpec(memory_space=pltpu.VMEM)
    return pl.pallas_call(
        kernel,
        in_specs=[far] * counts[0] + [near] * counts[1],
        out_specs=[far] * counts[2] + [near] * counts[3],
        out_shape=[jax.ShapeDtypeStruct(shape, jnp.float32) for shape, _ in out_streamed]
        + [pltpu.VMEM(shape, jnp.float32) for shape in out_kept],
        scratch_shapes=scratch,
        input_output_aliases={} if reused is None else {counts[0] + reused[0]: counts[2] + reused[1]},
        cost_estimate=pl.CostEstimate(flops=flops, bytes_accessed=moved, transcendentals=0),
        compiler_params=pltpu.CompilerParams(vmem_limit_bytes=grant * 1024 * 1024),
    )(
        *[placed(array) for array, _ in streamed],
        *[pltpu.with_memory_space_constraint(array, pltpu.VMEM) for array in kept],
    )


def state_rims_body(first, second, packed, low, high):
    rows = first.shape[1]
    lane = lane_of(rows)
    owner = lane // GROUP
    spot = lane % GROUP

    def plane(base, part, edge):
        i = base + part
        a = first[i].astype(jnp.float32)
        b = second[i].astype(jnp.float32)
        low[0, pl.ds(i, 1), :] = a[:1]
        low[1, pl.ds(i, 1), :] = b[:1]
        high[0, pl.ds(i, 1), :] = a[rows - 1 :]
        high[1, pl.ds(i, 1), :] = b[rows - 1 :]
        both = jnp.where(spot < 2, turned_to(a, GROUP * part + 1), turned_to(b, GROUP * part + 3))
        return jnp.where(owner == part, both, edge)

    for b in range(LONG // PART):
        packed[:, b * LANES : (b + 1) * LANES] = planes_loop(
            PART, functools.partial(plane, b * PART), jnp.zeros((rows, LANES), jnp.float32), PART
        )


def state_rims(first, second):
    xlen, rows = first.shape[0], first.shape[1]
    block = pl.BlockSpec((LONG, rows, LANES), lambda i: (i, 0, 0))
    slab = pl.BlockSpec((2, LONG, LANES), lambda i: (0, i, 0))
    return call(
        state_rims_body,
        (xlen // LONG,),
        [(first, block), (second, block)],
        [],
        [
            ((rows, GROUP * xlen), pl.BlockSpec((rows, LONG // PART * LANES), lambda i: (0, i))),
            ((2, xlen, LANES), slab),
            ((2, xlen, LANES), slab),
        ],
        [],
        [],
        8 * first.size,
        4 * first.size,
    )


def stencil_table():
    cell = np.arange(LANES)
    gap = np.abs(cell[:, None] - cell[None, :])
    outer = np.where(gap == 0, 38.0, np.where(gap == 1, -12.0, np.where(gap == 2, 1.0, 0.0)))
    inner = np.where(gap == 0, -12.0, np.where(gap == 1, 2.0, 0.0))
    table = np.concatenate([outer, inner], axis=1)
    return doubled(table)


def stencil_body(
    before, cells, after, table, packed, low, high, low_curve, high_curve, out, padded, inner
):
    rows = cells.shape[2]
    comp = pl.program_id(0)
    base = pl.program_id(1) * LONG
    owner = lane_of(rows) // GROUP
    here = pl.ds(TOP, rows)

    @pl.when((comp == 0) & (base == 0))
    def _():
        padded[...] = jnp.zeros_like(padded)

    for j in range(2):
        padded[j, here] = before[0, j]
        padded[LONG + 2 + j, here] = after[0, j]

    def fill(i, carry):
        padded[i + 2, here] = cells[0, i]
        return carry

    planes_loop(LONG, fill)

    def middle(j, count):
        flat = padded[pl.ds(j, count), here].reshape(count * rows, LANES)
        both = product(halves(flat), table[...])
        found = []
        for k in range(count):
            value = padded[j + k, here]
            part = both[k * rows : (k + 1) * rows]
            along = padded[j + k - 1, here] + padded[j + k + 1, here]
            core = (
                part[:, LANES:]
                + along
                + (padded[j + k, pl.ds(TOP - 1, rows)] + padded[j + k, pl.ds(TOP + 1, rows)])
            )
            inner[j + k - 1, here] = core
            inner[j + k - 1, TOP - 1 : TOP] = value[:1]
            inner[j + k - 1, TOP + rows : TOP + rows + 1] = value[rows - 1 :]
            found.append((value, part[:, :LANES], core, along))
        return found

    middle(1, 1)
    middle(LONG + 2, 1)

    for b in range(LONG // PART):

        def several(k, edge):
            first = b * PART + k * BATCH
            for j, (value, outer, core, along) in enumerate(middle(first + 2, BATCH)):
                i = first + j
                out[comp, base + i] = GAMMA * value + BETA * outer
                low[0, pl.ds(i, 1), :] = value[:1]
                high[0, pl.ds(i, 1), :] = value[rows - 1 :]
                low_curve[0, pl.ds(i, 1), :] = core[:1] + along[:1]
                high_curve[0, pl.ds(i, 1), :] = core[rows - 1 :] + along[rows - 1 :]
                part = k * BATCH + j
                edge = jnp.where(owner == part, turned_to(value, GROUP * part + 2), edge)
            return edge

        packed[0, :, b * LANES : (b + 1) * LANES] = lax.fori_loop(
            0, PART // BATCH, several, jnp.zeros((rows, LANES), jnp.float32)
        )

    def finish(i, carry):
        around = (inner[i, here] + inner[i + 2, here]) + (
            inner[i + 1, pl.ds(TOP - 1, rows)] + inner[i + 1, pl.ds(TOP + 1, rows)]
        )
        out[comp, base + i] = out[comp, base + i] + BETA * around
        return carry

    planes_loop(LONG, finish)


def stencil(increment, table):
    parts, xlen, rows = increment.shape[:3]
    half = LONG // 2
    pairs = xlen // 2
    slab = pl.BlockSpec((1, LONG, LANES), lambda c, i: (c, i, 0))
    return call(
        stencil_body,
        (parts, xlen // LONG),
        [
            (
                increment,
                pl.BlockSpec(
                    (1, 2, rows, LANES),
                    lambda c, i: (c, lax.rem(half * i + pairs - 1, pairs), 0, 0),
                ),
            ),
            (increment, pl.BlockSpec((1, LONG, rows, LANES), lambda c, i: (c, i, 0, 0))),
            (
                increment,
                pl.BlockSpec(
                    (1, 2, rows, LANES), lambda c, i: (c, lax.rem(half * i + half, pairs), 0, 0)
                ),
            ),
        ],
        [table],
        [
            (
                (parts, rows, GROUP * xlen),
                pl.BlockSpec((1, rows, LONG // PART * LANES), lambda c, i: (c, 0, i)),
            ),
        ]
        + [((parts, xlen, LANES), slab)] * 4,
        [increment.shape],
        [
            pltpu.VMEM((LONG + 4, rows + 2 * TOP, LANES), jnp.float32),
            pltpu.VMEM((LONG + 2, rows + 2 * TOP, LANES), jnp.float32),
        ],
        24 * increment.size,
        4 * increment.size,
        12,
    )


def corner_table():
    table = np.zeros((LANES, LANES))
    table[1::GROUP, 0] = 2.0
    table[2::GROUP, LANES - 1] = 2.0
    return table


def corner_body(low, high, left, right, table, out_low, out_high):
    parts, xlen = low.shape[:2]
    rows = left.shape[1]
    row = lax.broadcasted_iota(jnp.int32, (PART, LANES), 0)
    lane = lax.broadcasted_iota(jnp.int32, (PART, LANES), 1)
    mine = lane // GROUP == row
    for c in range(parts):
        for b in range(xlen // PART):
            planes = slice(b * PART, (b + 1) * PART)
            lanes = slice(b * LANES, (b + 1) * LANES)
            for curve, out, at in ((low, out_low, 0), (high, out_high, rows - 1)):
                rim = jnp.where(
                    lane % GROUP == 1, left[c, at : at + 1, lanes], right[c, at : at + 1, lanes]
                )
                rim = halves(jnp.where(mine, rim, 0.0))
                out[c, planes] = BETA * (curve[c, planes] + product(rim, table[...]))


def corners(low, high, left, right):
    near = pl.BlockSpec(memory_space=pltpu.VMEM)
    return pl.pallas_call(
        corner_body,
        in_specs=[near] * 5,
        out_specs=[near] * 2,
        out_shape=[jax.ShapeDtypeStruct(low.shape, jnp.float32)] * 2,
        cost_estimate=pl.CostEstimate(
            flops=8 * low.size, bytes_accessed=16 * low.size, transcendentals=0
        ),
        compiler_params=pltpu.CompilerParams(vmem_limit_bytes=12 * 1024 * 1024),
    )(low, high, left, right, doubled(corner_table()))


def edges_body(
    low, high, low_curve, high_curve, lanes, filtered, out,
):
    rows = filtered.shape[2]
    base = pl.program_id(0) * PART
    lane = lane_of(rows)
    row = lax.broadcasted_iota(jnp.int32, (8, LANES), 0)
    outer = (lane < 2) | (lane >= LANES - 2)
    for d in range(3):

        def plane(i, carry):
            at = pl.ds(i, 1)
            cyclic = turned_from(lanes[d], GROUP * i + 2)
            value = filtered[d, base + i] + jnp.where(outer, cyclic, 0.0)
            first = jnp.where(row == 1, BETA * low[d, at], 0.0)
            first = jnp.where(row == 0, low_curve[d, at], first)
            last = jnp.where(row == 6, BETA * high[d, at], 0.0)
            last = jnp.where(row == 7, high_curve[d, at], last)
            if rows == 8:
                out[d, base + i] = value + first + last
            else:
                out[d, base + i, :8] = value[:8] + first
                out[d, base + i, 8 : rows - 8] = value[8 : rows - 8]
                out[d, base + i, rows - 8 :] = value[rows - 8 :] + last
            return carry

        planes_loop(PART, plane, 0, 32)


def edges_pass(filtered, low, high, low_curve, high_curve, lanes):
    parts, xlen, rows = filtered.shape[:3]
    slab = pl.BlockSpec((parts, PART, LANES), lambda i: (0, i, 0))
    return call(
        edges_body,
        (xlen // PART,),
        [(low, slab), (high, slab), (low_curve, slab), (high_curve, slab)]
        + [(lanes, pl.BlockSpec((parts, rows, LANES), lambda i: (0, 0, i)))],
        [filtered],
        [],
        [filtered.shape],
        [],
        4 * filtered.size,
        filtered.size,
        4,
        (0, 0),
    )[0]


def gradient_table():
    cell = np.arange(LANES)
    gap = cell[None, :] - cell[:, None]
    slope = (gap == -1).astype(np.float64) - (gap == 1)
    none = np.zeros_like(slope)
    rims = np.zeros((LANES, 2 * LANES))
    rims[0::GROUP, 0] = -1.0
    rims[1::GROUP, LANES - 1] = 1.0
    rims[2::GROUP, LANES] = -1.0
    rims[3::GROUP, 2 * LANES - 1] = 1.0
    return jnp.asarray(np.block([[slope, none], [none, slope], [rims]]), jnp.bfloat16)


def load_states(m0, m0b, m0a, m1, m1b, m1a, lows, highs, rims, table, pad0, pad1, slopes):
    rows = m0.shape[1]
    base = pl.program_id(0) * PART
    here = pl.ds(TOP, rows)
    owner = lane_of(rows) // GROUP
    for which, (ref, before, after, pad) in enumerate(((m0, m0b, m0a, pad0), (m1, m1b, m1a, pad1))):

        @pl.when(base == 0)
        def _():
            pad[0, here] = before[0].astype(jnp.float32)

        pad[base + PART + 1, here] = after[0].astype(jnp.float32)

        def fill(i, carry):
            pad[base + i + 1, here] = ref[i].astype(jnp.float32)
            pad[base + i + 1, pl.ds(TOP - 1, 1)] = lows[which, pl.ds(i, 1), :]
            pad[base + i + 1, pl.ds(TOP + rows, 1)] = highs[which, pl.ds(i, 1), :]
            return carry

        planes_loop(PART, fill)

    def several(k, carry):
        first = k * BATCH
        flat = [
            pad[pl.ds(base + first + 1, BATCH), here].reshape(BATCH * rows, LANES).astype(jnp.bfloat16)
            for pad in (pad0, pad1)
        ]
        edge = jnp.concatenate([jnp.where(owner == first + j, rims, 0.0) for j in range(BATCH)], axis=0)
        both = product(jnp.concatenate(flat + [edge.astype(jnp.bfloat16)], axis=1), table[...])
        slopes[pl.ds(base + first, BATCH)] = both.reshape(BATCH, rows, 2 * LANES)
        return carry

    lax.fori_loop(0, PART // BATCH, several, 0)


def gradients(pad, slope, i, rows):
    here = pl.ds(TOP, rows)
    return (
        pad[i + 2, here] - pad[i, here],
        pad[i + 1, pl.ds(TOP + 1, rows)] - pad[i + 1, pl.ds(TOP - 1, rows)],
        slope,
    )


def crossed_rims(left, right, rows):
    rims = merged_rims(left, right, rows)
    return jnp.where(lane_of(rows) % 2 == 0, turn(rims, -1), turn(rims, 1))


def merged_rims(left, right, rows):
    spot = lane_of(rows) % GROUP
    return jnp.where(spot % 2 == 0, left[...], right[...])


def first_state_body(
    increment, m0, m0b, m0a, m1, m1b, m1a, lows, highs, left, right, table,
    packed, low, high, state, source, pad0, pad1, slopes,
):
    rows = m0.shape[1]
    base = pl.program_id(0) * PART
    owner = lane_of(rows) // GROUP
    rims = merged_rims(left, right, rows)
    load_states(m0, m0b, m0a, m1, m1b, m1a, lows, highs, rims, table, pad0, pad1, slopes)

    def plane(i, edge):
        g0 = gradients(pad0, slopes[base + i, :, :LANES], base + i, rows)
        g1 = gradients(pad1, slopes[base + i, :, LANES:], base + i, rows)
        u = [increment[d, i] for d in range(3)]
        one = (-0.5 * STEP) * (u[0] * g0[0] + u[1] * g0[1] + u[2] * g0[2])
        state[base + i] = one
        source[base + i] = (0.5 * STEP) * (u[0] * g1[0] + u[1] * g1[1] + u[2] * g1[2])
        low[pl.ds(i, 1), :] = one[:1]
        high[pl.ds(i, 1), :] = one[rows - 1 :]
        return jnp.where(owner == i, turned_to(one, GROUP * i + 1), edge)

    packed[...] = planes_loop(PART, plane, jnp.zeros((rows, LANES), jnp.float32), 32)


def around(array):
    xlen, rows = array.shape[:2]
    return [
        (array, pl.BlockSpec((PART, rows, LANES), lambda i: (i, 0, 0))),
        (array, pl.BlockSpec((1, rows, LANES), lambda i: (lax.rem(PART * i + xlen - 1, xlen), 0, 0))),
        (array, pl.BlockSpec((1, rows, LANES), lambda i: (lax.rem(PART * i + PART, xlen), 0, 0))),
    ]


def first_state(increment, first, second, lows, highs, left, right):
    xlen, rows = first.shape[0], first.shape[1]
    triple = pl.BlockSpec((3, PART, rows, LANES), lambda i: (0, i, 0, 0))
    slab = pl.BlockSpec((PART, LANES), lambda i: (i, 0))
    double = pl.BlockSpec((2, PART, LANES), lambda i: (0, i, 0))
    rim = pl.BlockSpec((rows, LANES), lambda i: (0, i))
    return call(
        first_state_body,
        (xlen // PART,),
        [(increment, triple)]
        + around(first)
        + around(second)
        + [(lows, double), (highs, double), (left, rim), (right, rim)],
        [gradient_table()],
        [((rows, GROUP * xlen), rim), ((xlen, LANES), slab), ((xlen, LANES), slab)],
        [first.shape, first.shape]
        + [(xlen + 2, rows + 2 * TOP, LANES)] * 2
        + [(xlen, rows, 2 * LANES)],
        [],
        24 * first.size,
        16 * first.size,
        6,
    )


def second_state_body(
    velocity, low, high, left, right, state, source, packed, out_low, out_high, adjoint, across
):
    xlen, rows = state.shape[0], state.shape[1]
    base = pl.program_id(0) * PART
    lane = lane_of(rows)
    owner = lane // GROUP
    rims = crossed_rims(left, right, rows)

    def lanes_part(i, carry):
        value = state[base + i]
        speed = velocity[2, i]
        before, after = z_sides(value, turned_from(rims, GROUP * i + 1), lane)
        across[i] = (STEP * speed) * jnp.where(speed > 0.0, value - before, after - value)
        return carry

    planes_loop(PART, lanes_part, 0, 32)

    def plane(i, edge):
        value = state[base + i]
        total = (source[base + i] - value) + across[i]
        sides = [
            (
                state[lax.rem(base + i + xlen - 1, xlen)],
                state[lax.rem(base + i + 1, xlen)],
            ),
            y_sides(value, low[pl.ds(i, 1), :], high[pl.ds(i, 1), :]),
        ]
        for d in range(2):
            speed = velocity[d, i]
            slope = jnp.where(speed > 0.0, value - sides[d][0], sides[d][1] - value)
            total = total + (STEP * speed) * slope
        adjoint[base + i] = total
        along = velocity[1, i]
        out_low[pl.ds(i, 1), :] = jnp.maximum(along[:1], 0.0) * total[:1]
        out_high[pl.ds(i, 1), :] = jnp.minimum(along[rows - 1 :], 0.0) * total[rows - 1 :]
        along = velocity[2, i]
        flow = total * jnp.where(
            lane == LANES - 1, jnp.minimum(along, 0.0), jnp.maximum(along, 0.0)
        )
        return jnp.where(owner == i, turned_to(flow, GROUP * i + 1), edge)

    packed[...] = planes_loop(PART, plane, jnp.zeros((rows, LANES), jnp.float32), 32)


def second_state(velocity, source, state, low, high, left, right):
    xlen, rows = state.shape[0], state.shape[1]
    triple = pl.BlockSpec((3, PART, rows, LANES), lambda i: (0, i, 0, 0))
    slab = pl.BlockSpec((PART, LANES), lambda i: (i, 0))
    rim = pl.BlockSpec((rows, LANES), lambda i: (0, i))
    return call(
        second_state_body,
        (xlen // PART,),
        [(velocity, triple), (low, slab), (high, slab), (left, rim), (right, rim)],
        [state, source],
        [((rows, GROUP * xlen), rim), ((xlen, LANES), slab), ((xlen, LANES), slab)],
        [state.shape],
        [pltpu.VMEM((PART, rows, LANES), jnp.float32)],
        30 * state.size,
        12 * state.size,
        6,
        (1, 0),
    )


def fold_table(count):
    return np.repeat(np.eye(count), 4, axis=1)


def hessian_body(
    velocity, speed_b, speed_a, flow_low, flow_high, flow_left, flow_right,
    filtered, adjoint, pad0, pad1, slopes, fold_z, out, restricted, flows, sums, few,
):
    xlen, rows = adjoint.shape[0], adjoint.shape[1]
    base = pl.program_id(0) * PART
    lane = lane_of(rows)
    row = lax.broadcasted_iota(jnp.int32, (rows, LANES), 0)
    ends = crossed_rims(flow_left, flow_right, rows)

    def across(i, carry):
        value = adjoint[base + i]
        speed = velocity[2, i]
        rim = turned_from(ends, GROUP * i + 1)
        later = turn(jnp.maximum(speed, 0.0) * value, -1)
        prev = turn(jnp.minimum(speed, 0.0) * value, 1)
        flows[i] = jnp.where(lane == LANES - 1, rim, later) - jnp.where(lane == 0, rim, prev)
        return carry

    planes_loop(PART, across, 0, 32)

    def plane(i, carry):
        g0 = gradients(pad0, slopes[base + i, :, :LANES], base + i, rows)
        g1 = gradients(pad1, slopes[base + i, :, LANES:], base + i, rows)
        value = adjoint[base + i]
        sx, sy, sz = (velocity[d, i] for d in range(3))
        before, after = jnp.maximum(i - 1, 0), jnp.minimum(i + 1, PART - 1)
        speed_before = jnp.where(i == 0, speed_b[0, 0], velocity[0, before])
        speed_after = jnp.where(i == PART - 1, speed_a[0, 0], velocity[0, after])
        prev = jnp.minimum(speed_before, 0.0) * adjoint[lax.rem(base + i + xlen - 1, xlen)]
        later = jnp.maximum(speed_after, 0.0) * adjoint[lax.rem(base + i + 1, xlen)]
        inflow = pltpu.roll(jnp.minimum(sy, 0.0) * value, 1, 0)
        outflow = pltpu.roll(jnp.maximum(sy, 0.0) * value, rows - 1, 0)
        change = (
            (later - prev)
            + flows[i]
            + jnp.where(row == rows - 1, flow_high[pl.ds(i, 1), :], outflow)
            - jnp.where(row == 0, flow_low[pl.ds(i, 1), :], inflow)
            - (jnp.abs(sx) + jnp.abs(sy) + jnp.abs(sz)) * value
        )
        half_two = (0.5 * STEP) * value
        half_one = half_two + (0.5 * STEP * STEP) * change
        for d in range(3):
            out[d, i] = filtered[d, base + i] + half_one * g0[d] + half_two * g1[d]
        return carry

    planes_loop(PART, plane, 0, 16)

    count = PART // 4 * (rows // 4)
    for d in range(3):

        def fold(k, carry):
            total = (out[d, 4 * k] + out[d, 4 * k + 1]) + (out[d, 4 * k + 2] + out[d, 4 * k + 3])
            total = total + pltpu.roll(total, rows - 1, 0)
            sums[pl.ds(k * rows, rows)] = total + pltpu.roll(total, rows - 2, 0)
            return carry

        planes_loop(PART // 4, fold)
        few[pl.ds(d * count, count)] = sums[pl.ds(0, count, stride=4)]
    found = product(halves(few[...]), fold_z[...]) * (1.0 / 64.0)
    restricted[...] = found.reshape(3, count, LANES // 4)


def hessian_pass(
    filtered, velocity, adjoint, pads, flow_low, flow_high, flow_left, flow_right,
):
    xlen, rows = adjoint.shape[0], adjoint.shape[1]
    triple = pl.BlockSpec((3, PART, rows, LANES), lambda i: (0, i, 0, 0))
    slab = pl.BlockSpec((PART, LANES), lambda i: (i, 0))
    rim = pl.BlockSpec((rows, LANES), lambda i: (0, i))
    speed_b = pl.BlockSpec(
        (1, 1, rows, LANES), lambda i: (0, lax.rem(PART * i + xlen - 1, xlen), 0, 0)
    )
    speed_a = pl.BlockSpec((1, 1, rows, LANES), lambda i: (0, lax.rem(PART * i + PART, xlen), 0, 0))
    coarse_rows = PART // 4 * (rows // 4)
    return call(
        hessian_body,
        (xlen // PART,),
        [(velocity, triple), (velocity, speed_b), (velocity, speed_a)]
        + [(flow_low, slab), (flow_high, slab), (flow_left, rim), (flow_right, rim)],
        [filtered, adjoint, *pads, doubled(fold_table(LANES // 4).T)],
        [
            (filtered.shape, triple),
            (
                (3, xlen // 4 * (rows // 4), LANES // 4),
                pl.BlockSpec((3, coarse_rows, LANES // 4), lambda i: (0, i, 0)),
            ),
        ],
        [],
        [
            pltpu.VMEM((PART, rows, LANES), jnp.float32),
            pltpu.VMEM((PART // 4 * rows, LANES), jnp.float32),
            pltpu.VMEM((3 * coarse_rows, LANES), jnp.float32),
        ],
        70 * adjoint.size,
        24 * adjoint.size,
        9,
    )


def final_body(coarse, hessian, spread_z, out, wide):
    rows = hessian.shape[2]
    few = rows // 4
    wide[...] = product(halves(coarse[0]), spread_z[...])
    half = lax.broadcasted_iota(jnp.int32, (8, LANES), 0) < 4

    def fold(k, carry):
        add = [
            jnp.where(
                half, wide[pl.ds(k * few + 2 * r, 1), :], wide[pl.ds(k * few + 2 * r + 1, 1), :]
            )
            for r in range(rows // 8)
        ]
        add = jnp.concatenate(add, axis=0)
        for j in range(4):
            out[0, 4 * k + j] = OMEGA * hessian[0, 4 * k + j] + add
        return carry

    planes_loop(WIDE // 4, fold, 0, 2)


def final_pass(hessian, coarse):
    parts, xlen, rows = hessian.shape[:3]
    block = pl.BlockSpec((1, WIDE, rows, LANES), lambda c, i: (c, i, 0, 0))
    coarse_rows = WIDE // 4 * (rows // 4)
    return call(
        final_body,
        (parts, xlen // WIDE),
        [
            (coarse, pl.BlockSpec((1, coarse_rows, LANES // 4), lambda c, i: (c, i, 0))),
            (hessian, block),
        ],
        [doubled(fold_table(LANES // 4))],
        [(hessian.shape, block)],
        [],
        [pltpu.VMEM((coarse_rows, LANES), jnp.float32)],
        2 * hessian.size,
        8 * hessian.size,
        20,
    )[0]


def coarse_spread(restricted):
    both = ("gz", "gy")
    groups_z = lax.axis_size("gz")
    groups_y = lax.axis_size("gy")
    devices = groups_z * groups_y
    cxlen, cylen, czlen = (restricted.shape[1], restricted.shape[2], restricted.shape[3])
    full_y = groups_y * cylen
    full_z = groups_z * czlen
    each = -(-3 * cxlen // devices)
    table_x = cas_table(cxlen)
    table_y = cas_table(full_y)
    table_z = cas_table(full_z)
    coeffs = jnp.einsum("xi,cijk->cxjk", table_x, restricted, precision=HIGH)
    coeffs = coeffs.reshape(3 * cxlen, cylen, czlen)
    coeffs = jnp.pad(coeffs, ((0, each * devices - 3 * cxlen), (0, 0), (0, 0)))
    planes = lax.all_to_all(coeffs, both, 0, 0, tiled=True)
    planes = planes.reshape(groups_z, groups_y, each, cylen, czlen)
    planes = planes.transpose(2, 1, 3, 0, 4).reshape(each, full_y, full_z)
    planes = jnp.einsum("yj,pjk->pyk", table_y, planes, precision=HIGH)
    planes = jnp.einsum("zk,pyk->pyz", table_z, planes, precision=HIGH)
    line_x = jnp.tile(eigen_line(cxlen), -(-each * devices // cxlen))
    line_x = lax.dynamic_slice_in_dim(line_x, lax.axis_index(both) * each, each, 0)
    total = (
        line_x[:, None, None] + eigen_line(full_y)[None, :, None] + eigen_line(full_z)[None, None, :]
    )
    planes = planes / (GAMMA + COARSE_BETA * total * total)
    planes = jnp.einsum("zk,pyk->pyz", table_z, planes, precision=HIGH)
    planes = jnp.einsum("yj,pjk->pyk", table_y, planes, precision=HIGH)
    planes = planes.reshape(each, groups_y, cylen, groups_z, czlen).transpose(3, 1, 0, 2, 4)
    planes = planes.reshape(devices * each, cylen, czlen)
    coeffs = lax.all_to_all(planes, both, 0, 0, tiled=True)[: 3 * cxlen]
    coeffs = coeffs.reshape(3, cxlen, cylen, czlen)
    coeffs = jnp.einsum("xi,cijk->cxjk", table_x, coeffs, precision=HIGH)
    return coeffs / float(cxlen * full_y * full_z)


def lane_curve(left, right):
    spot = lax.broadcasted_iota(jnp.int32, left.shape, 2) % GROUP
    rims = jnp.where(spot < 2, left, right)
    rows = rims.shape[1]
    empty = jnp.zeros_like(rims[:, :1])
    up = jnp.concatenate([rims[:, 1:], empty], axis=1)
    down = jnp.concatenate([empty, rims[:, : rows - 1]], axis=1)
    bent = -2.0 * (
        6.0 * rims - jnp.roll(rims, GROUP, 2) - jnp.roll(rims, -GROUP, 2) - up - down
    )
    plain = jnp.where(spot < 2, jnp.roll(rims, -2, 2), jnp.roll(rims, 2, 2))
    curve = jnp.where(spot == 1, jnp.roll(bent, -1, 2), jnp.roll(bent, 1, 2))
    return BETA * (plain + jnp.where((spot == 1) | (spot == 2), curve, 0.0))


def per_device(velocity, increment, template, deformed):
    xlen, rows = template.shape[0], template.shape[1]

    packed, low, high = state_rims(template, deformed)
    packed, low, high, table = lax.optimization_barrier((packed, low, high, stencil_table()))
    left = shifted(packed, "gz", 1)
    right = shifted(packed, "gz", -1)
    lows = shifted(high, "gy", 1)
    highs = shifted(low, "gy", -1)

    inc_packed, inc_low, inc_high, low_curve, high_curve, filtered = stencil(increment, table)
    inc_packed, inc_low, inc_high, left, right, lows, highs = lax.optimization_barrier(
        (inc_packed, inc_low, inc_high, left, right, lows, highs)
    )
    inc_left = shifted(inc_packed, "gz", 1)
    inc_right = shifted(inc_packed, "gz", -1)
    inc_lows = shifted(inc_high, "gy", 1)
    inc_highs = shifted(inc_low, "gy", -1)

    s_packed, s_low, s_high, state, source, *pads = first_state(
        increment, template, deformed, lows, highs, left, right
    )
    s_left = shifted(s_packed, "gz", 1)
    s_right = shifted(s_packed, "gz", -1)
    s_below = shifted(s_high, "gy", 1)
    s_above = shifted(s_low, "gy", -1)

    inc_left, inc_right, inc_lows, inc_highs = lax.optimization_barrier(
        (inc_left, inc_right, inc_lows, inc_highs)
    )
    low_curve, high_curve = corners(low_curve, high_curve, inc_left, inc_right)
    s_left, s_right, s_below, s_above, low_curve, high_curve = lax.optimization_barrier(
        (s_left, s_right, s_below, s_above, low_curve, high_curve)
    )
    low_curves = shifted(high_curve, "gy", 1)
    high_curves = shifted(low_curve, "gy", -1)

    f_packed, f_low, f_high, adjoint = second_state(
        velocity, source, state, s_below, s_above, s_left, s_right
    )
    f_packed, low_curves = lax.optimization_barrier((f_packed, low_curves))
    f_left = shifted(f_packed, "gz", 1)
    f_right = shifted(f_packed, "gz", -1)
    f_below = shifted(f_high, "gy", 1)
    f_above = shifted(f_low, "gy", -1)

    filtered = edges_pass(
        filtered, inc_lows, inc_highs, low_curves, high_curves, lane_curve(inc_left, inc_right)
    )
    hessian, restricted = hessian_pass(
        filtered, velocity, adjoint, pads, f_below, f_above, f_left, f_right
    )
    coarse = coarse_spread(restricted.reshape(3, xlen // 4, rows // 4, LANES // 4))
    mixed = coarse.reshape(restricted.shape) - OMEGA * restricted
    return final_pass(hessian, mixed)


def solution(mesh):
    placed = (
        P(None, None, "gy", "gz"),
        P(None, None, "gy", "gz"),
        P(None, "gy", "gz"),
        P(None, "gy", "gz"),
    )
    return jax.shard_map(
        per_device, mesh=mesh, in_specs=placed, out_specs=P(None, None, "gy", "gz"), check_vma=False
    )
```
